128 devices in a mesh: grp: 4 (over x_lo, core), sub: 32 (over y, z, x_hi).
Axes of the slice: x: 4 (x_hi: 2, x_lo: 2; x = x_hi * 2 + x_lo), y: 4, z: 4, core: 2. Of those that a mesh axis runs over, the one named last changes fastest.
Arguments:
- states: bfloat16 [524288, 128], P(('grp', 'sub')), may hold values from -6 to 6
- cotangent: bfloat16 [524288, 128], P(('grp', 'sub')), may hold values from -6 to 6
- fine_self: bfloat16 [128, 128], replicated, may hold values from -0.5 to 0.5
- fine_other: bfloat16 [128, 128], replicated, may hold values from -0.5 to 0.5
- fine_node: bfloat16 [128, 128], replicated, may hold values from -0.375 to 0.375
- coarse_self: bfloat16 [128, 128], replicated, may hold values from -0.5 to 0.5
- coarse_other: bfloat16 [128, 128], replicated, may hold values from -0.5 to 0.5
- coarse_node: bfloat16 [128, 128], replicated, may hold values from -0.375 to 0.375
- prolong: bfloat16 [128, 128], replicated, may hold values from -0.5 to 0.5
- fine_nbr: int32 [524288, 8], P(('grp', 'sub')), may hold values from 0 to 5119, as said below
- fine_mask: int32 [524288, 8], P(('grp', 'sub')), may hold values 0 or 1
- fine_send_lo: int32 [65536], P(('grp', 'sub')), may hold values from 0 to 4095
- fine_send_hi: int32 [65536], P(('grp', 'sub')), may hold values from 0 to 4095
- coarse_nbr: int32 [32768, 8], P('sub'), may hold values from 0 to 1151, as said below
- coarse_mask: int32 [32768, 8], P('sub'), may hold values 0 or 1
- coarse_send_lo: int32 [2048], P('sub'), may hold values from 0 to 1023
- coarse_send_hi: int32 [2048], P('sub'), may hold values from 0 to 1023
- coarse_owner: int32 [524288], P(('grp', 'sub')), may hold values from 0 to 1023, as said below
Outputs:
- result: bfloat16 [524288, 128], P(('grp', 'sub'))
- grad_states: bfloat16 [524288, 128], P(('grp', 'sub'))
- grad_weights: float32 [7, 128, 128], replicated
The draws below stay inside these ranges and needn't reach their ends.
Inputs may be any that keep to these rules, and one draw needn't show every extreme that they name: `coarse_owner`: on the devices of grp index 0 every mid-level cell is named by exactly 4096 // 1024 fine cells of that device; elsewhere names are drawn freely. `fine_nbr`: with B = 64, local row r of a device lies in block b = r // B; each of its slots names a row of block b of the local rows (b * B to b * B + B - 1), or row 4096 + (b % 8) * B + j, or row 4608 + (b % 8) * B + j, for some j below B. `coarse_nbr`: local row r of a partition lies in block b = r // 64; each of its slots names a row of block b of the local rows, or any of the 128 halo rows of the table.
All inputs are finite; a program needn't handle non-finite values. No bound on the sum of `fine_mask` or of `coarse_mask` on one device may be relied on, other than what follows from the above.
Results may differ from the reference program's by a relative error of at most 0.015.
Values may be sent and summed in bfloat16 or wider, within the bound.
A program may use at most 128 MiB of HBM per device.

```python
import jax
import jax.numpy as jnp
from jax import lax

D = 128
K = 8
NF_DEV = 4096
NC_DEV = 1024
HALO = 512
HALO_C = 64
NF = 524288
NC = 32768
N_GRP = 4
N_SUB = 32


def local_slots(key, rows_dev, halo_rows, block_rows, devices):
    total_rows = rows_dev * devices
    positions = jnp.arange(total_rows, dtype=jnp.int32)
    local_row = positions % rows_dev
    block_index = local_row // block_rows
    halo_blocks = halo_rows // block_rows
    halo_index = block_index % halo_blocks
    picks = jax.random.randint(key, (total_rows, K), 0, 3 * block_rows).astype(jnp.int32)
    base_local = (block_index * block_rows)[:, None]
    base_low = (rows_dev + halo_index * block_rows)[:, None]
    base_high = (rows_dev + halo_rows + halo_index * block_rows)[:, None]
    chosen = jnp.where(picks < block_rows, base_local + picks, jnp.where(picks < 2 * block_rows, base_low + picks - block_rows, base_high + picks - 2 * block_rows))
    return chosen.astype(jnp.int32)


def draw_fine_nbr(key, part):
    key = jax.random.fold_in(key, 11)
    return local_slots(key, NF_DEV, HALO, NF_DEV // 64, N_GRP * N_SUB)


def draw_coarse_nbr(key, part):
    key = jax.random.fold_in(key, 13)
    return local_slots(key, NC_DEV, HALO_C, HALO_C, N_SUB)


def draw_coarse_owner(key, part):
    key = jax.random.fold_in(key, 5)
    total_rows = NF_DEV * N_GRP * N_SUB
    positions = jnp.arange(total_rows, dtype=jnp.int32)
    local_row = positions % NF_DEV
    device_part = positions // NF_DEV % N_SUB
    group_index = positions // (NF_DEV * N_SUB)
    part_keys = jax.random.split(key, N_SUB)
    orders = jax.vmap(lambda single: jax.random.permutation(single, NF_DEV))(part_keys)
    covered = orders[device_part, local_row] % NC_DEV
    drawn = jax.random.randint(jax.random.fold_in(key, 1), (total_rows,), 0, NC_DEV)
    return jnp.where(group_index == 0, covered, drawn).astype(jnp.int32)


def touch_ends(array, key, smallest, top_value):
    longest = array.shape.index(max(array.shape))
    spots = []
    for shift in (0, 1):
        where = [jax.random.randint(jax.random.fold_in(key, axis), (), 0, length) for axis, length in enumerate(array.shape)]
        where[longest] = (where[longest] + shift) % array.shape[longest]
        spots.append(tuple(where))
    return array.at[spots[0]].set(smallest).at[spots[1]].set(top_value)


def block_levels(stream_key, extent, cuts, smallest, largest):
    gain = 1.0
    for dim, blocks in cuts:
        draws = jax.random.uniform(jax.random.fold_in(jax.random.fold_in(stream_key, 6), dim), (blocks,), jnp.float32, smallest / len(cuts), largest / len(cuts))
        gain = gain * jnp.repeat(jnp.exp(draws), extent[dim] // blocks).reshape((-1,) + (1,) * (len(extent) - 1 - dim))
    return gain


def noise(own_key, extent, deviation, most, shards=(), held_as=jnp.bfloat16):
    values = jax.random.normal(own_key, extent, jnp.float32) * deviation
    if len(shards) > 0:
        values = block_levels(own_key, extent, shards, -0.22, 0.18) * values
    return jnp.clip(values, min=-most, max=most).astype(held_as)


def setup_inputs(seed: int = 0) -> dict:
    splits = jax.random.split(jax.random.key(seed), 19)
    return {
        "states": noise(splits[0], (NF, D), 1.0, 6.0, ((0, 128),)),
        "cotangent": noise(splits[1], (NF, D), 1.0, 6.0, ((0, 128),)),
        "fine_self": noise(splits[2], (D, D), D ** -0.5, 0.5),
        "fine_other": noise(splits[3], (D, D), D ** -0.5, 0.5),
        "fine_node": noise(splits[4], (D, D), (2 * D) ** -0.5, 0.375),
        "coarse_self": noise(splits[5], (D, D), D ** -0.5, 0.5),
        "coarse_other": noise(splits[6], (D, D), D ** -0.5, 0.5),
        "coarse_node": noise(splits[7], (D, D), (2 * D) ** -0.5, 0.375),
        "prolong": noise(splits[8], (D, D), D ** -0.5, 0.5),
        "fine_nbr": draw_fine_nbr(jax.random.fold_in(splits[18], 71), 0),
        "fine_mask": touch_ends((jax.random.randint(splits[10], (NF, K), 0, 4) < 3).astype(jnp.int32), jax.random.fold_in(splits[10], 1), 0, 1),
        "fine_send_lo": touch_ends(jax.random.randint(splits[11], (N_GRP * N_SUB * HALO,), 0, NF_DEV), jax.random.fold_in(splits[11], 1), 0, NF_DEV - 1).astype(jnp.int32),
        "fine_send_hi": touch_ends(jax.random.randint(splits[12], (N_GRP * N_SUB * HALO,), 0, NF_DEV), jax.random.fold_in(splits[12], 1), 0, NF_DEV - 1).astype(jnp.int32),
        "coarse_nbr": draw_coarse_nbr(jax.random.fold_in(splits[18], 71), 0),
        "coarse_mask": touch_ends((jax.random.randint(splits[14], (NC, K), 0, 4) < 3).astype(jnp.int32), jax.random.fold_in(splits[14], 1), 0, 1),
        "coarse_send_lo": touch_ends(jax.random.randint(splits[15], (N_SUB * HALO_C,), 0, NC_DEV), jax.random.fold_in(splits[15], 1), 0, NC_DEV - 1).astype(jnp.int32),
        "coarse_send_hi": touch_ends(jax.random.randint(splits[16], (N_SUB * HALO_C,), 0, NC_DEV), jax.random.fold_in(splits[16], 1), 0, NC_DEV - 1).astype(jnp.int32),
        "coarse_owner": draw_coarse_owner(jax.random.fold_in(splits[18], 71), 0),
    }


highest = lax.Precision.HIGHEST


def halo_table(far_term, send_lo, send_hi):
    groups, parts = far_term.shape[0], far_term.shape[1]
    group_index = jnp.arange(groups)[:, None, None]
    part_index = jnp.arange(parts)[None, :, None]
    going_up = far_term[group_index, part_index, send_hi]
    going_down = far_term[group_index, part_index, send_lo]
    zero_rows = jnp.zeros_like(going_up[:, :1])
    from_lower = jnp.concatenate([zero_rows, going_up[:, :-1]], axis=1)
    from_upper = jnp.concatenate([going_down[:, 1:], zero_rows], axis=1)
    return jnp.concatenate([far_term, from_lower, from_upper], axis=2)


def edge_sum(own_term, table, neighbours, in_use):
    preact = own_term[:, None, :] + table[neighbours].astype(jnp.float32)
    return (jax.nn.silu(preact) * in_use[..., None].astype(jnp.float32)).sum(1).astype(jnp.bfloat16)


def edge_back(own_term, table, neighbours, in_use, grad_sum):
    preact = own_term[:, None, :] + table[neighbours].astype(jnp.float32)
    gate_value = jax.nn.sigmoid(preact)
    slope = gate_value * (1.0 + preact * (1.0 - gate_value))
    grad_pre = grad_sum[:, None, :] * in_use[..., None].astype(jnp.float32) * slope
    features = own_term.shape[1]
    grad_table = jax.ops.segment_sum(grad_pre.reshape(-1, features), neighbours.reshape(-1), num_segments=table.shape[0])
    return grad_pre.sum(1), grad_table


def level_forward(latents, w_self, w_other, w_node, neighbours, in_use, send_lo, send_hi):
    groups, parts, rows, features = latents.shape
    flat = latents.reshape(-1, features)
    own_term = jnp.dot(flat, w_self, preferred_element_type=jnp.float32).reshape(groups, parts, rows, features)
    far_term = jnp.dot(flat, w_other, preferred_element_type=jnp.float32).astype(jnp.bfloat16).reshape(groups, parts, rows, features)
    table = halo_table(far_term, send_lo, send_hi)
    table_rows = table.shape[2]
    summed = lax.map(lambda piece: edge_sum(*piece), (own_term.reshape(-1, rows, features), table.reshape(-1, table_rows, features), neighbours.reshape(-1, rows, neighbours.shape[-1]), in_use.reshape(-1, rows, neighbours.shape[-1])))
    summed = summed.reshape(groups, parts, rows, features)
    updated = flat.astype(jnp.float32) + jnp.dot(summed.reshape(-1, features), w_node, preferred_element_type=jnp.float32)
    return updated.reshape(groups, parts, rows, features), own_term, table, summed


def level_backward(latents, w_self, w_other, w_node, own_term, table, summed, neighbours, in_use, send_lo, send_hi, grad_up):
    groups, parts, rows, features = latents.shape
    halo_rows = send_lo.shape[2]
    grad_flat = grad_up.reshape(-1, features)
    grad_sum = jnp.dot(grad_flat, w_node.astype(jnp.float32).T, precision=highest)
    grad_node = jnp.dot(summed.reshape(-1, features).astype(jnp.float32).T, grad_flat, precision=highest)
    table_rows = table.shape[2]
    grad_own, grad_table = lax.map(lambda piece: edge_back(*piece), (own_term.reshape(-1, rows, features), table.reshape(-1, table_rows, features), neighbours.reshape(-1, rows, neighbours.shape[-1]), in_use.reshape(-1, rows, neighbours.shape[-1]), grad_sum.reshape(-1, rows, features)))
    grad_own = grad_own.reshape(groups, parts, rows, features)
    grad_table = grad_table.reshape(groups, parts, table_rows, features)
    lower_part = grad_table[:, :, rows:rows + halo_rows]
    upper_part = grad_table[:, :, rows + halo_rows:]
    zero_rows = jnp.zeros_like(lower_part[:, :1])
    back_down = jnp.concatenate([lower_part[:, 1:], zero_rows], axis=1)
    back_up = jnp.concatenate([zero_rows, upper_part[:, :-1]], axis=1)
    group_index = jnp.arange(groups)[:, None, None]
    part_index = jnp.arange(parts)[None, :, None]
    grad_far = grad_table[:, :, :rows]
    grad_far = grad_far.at[group_index, part_index, send_hi].add(back_down)
    grad_far = grad_far.at[group_index, part_index, send_lo].add(back_up)
    own_flat = grad_own.reshape(-1, features)
    far_flat = grad_far.reshape(-1, features)
    latent_flat = latents.reshape(-1, features).astype(jnp.float32)
    grad_self = jnp.dot(latent_flat.T, own_flat, precision=highest)
    grad_other = jnp.dot(latent_flat.T, far_flat, precision=highest)
    grad_latent = grad_flat + jnp.dot(own_flat, w_self.astype(jnp.float32).T, precision=highest) + jnp.dot(far_flat, w_other.astype(jnp.float32).T, precision=highest)
    return grad_latent, grad_self, grad_other, grad_node


def reference(states, cotangent, fine_self, fine_other, fine_node, coarse_self, coarse_other, coarse_node, prolong, fine_nbr, fine_mask, fine_send_lo, fine_send_hi, coarse_nbr, coarse_mask, coarse_send_lo, coarse_send_hi, coarse_owner):
    groups, parts = N_GRP, N_SUB
    features = states.shape[1]
    slots = fine_nbr.shape[1]
    fine_rows = states.shape[0] // (groups * parts)
    coarse_rows = coarse_nbr.shape[0] // parts
    latents = states.reshape(groups, parts, fine_rows, features)
    fine_n = fine_nbr.reshape(groups, parts, fine_rows, slots)
    fine_m = fine_mask.reshape(groups, parts, fine_rows, slots)
    fine_lo = fine_send_lo.reshape(groups, parts, -1)
    fine_hi = fine_send_hi.reshape(groups, parts, -1)
    updated, own_term, table, summed = level_forward(latents, fine_self, fine_other, fine_node, fine_n, fine_m, fine_lo, fine_hi)
    segment_ids = (jnp.arange(parts, dtype=jnp.int32)[None, :, None] * coarse_rows + coarse_owner.reshape(groups, parts, fine_rows)).reshape(-1).astype(jnp.int32)
    totals = jax.ops.segment_sum(updated.reshape(-1, features), segment_ids, num_segments=parts * coarse_rows)
    counts = jax.ops.segment_sum(jnp.ones(segment_ids.shape[0], jnp.float32), segment_ids, num_segments=parts * coarse_rows)
    coarse_in = (totals / counts[:, None]).astype(jnp.bfloat16).reshape(1, parts, coarse_rows, features)
    coarse_n = coarse_nbr.reshape(1, parts, coarse_rows, slots)
    coarse_m = coarse_mask.reshape(1, parts, coarse_rows, slots)
    coarse_lo = coarse_send_lo.reshape(1, parts, -1)
    coarse_hi = coarse_send_hi.reshape(1, parts, -1)
    coarse_up, coarse_own, coarse_table, coarse_sum = level_forward(coarse_in, coarse_self, coarse_other, coarse_node, coarse_n, coarse_m, coarse_lo, coarse_hi)
    coarse_out = coarse_up.astype(jnp.bfloat16).reshape(-1, features)
    picked = coarse_out[segment_ids]
    result = (updated.reshape(-1, features) + jnp.dot(picked, prolong, preferred_element_type=jnp.float32)).astype(jnp.bfloat16)
    grad_out = cotangent.astype(jnp.float32)
    grad_prolong = jnp.dot(picked.astype(jnp.float32).T, grad_out, precision=highest)
    grad_picked = jnp.dot(grad_out, prolong.astype(jnp.float32).T, precision=highest)
    grad_coarse = jax.ops.segment_sum(grad_picked, segment_ids, num_segments=parts * coarse_rows)
    grad_cin, grad_cself, grad_cother, grad_cnode = level_backward(coarse_in, coarse_self, coarse_other, coarse_node, coarse_own, coarse_table, coarse_sum, coarse_n, coarse_m, coarse_lo, coarse_hi, grad_coarse.reshape(1, parts, coarse_rows, features))
    grad_mean = grad_cin.reshape(-1, features) / counts[:, None]
    grad_updated = grad_out + grad_mean[segment_ids]
    grad_latent, grad_fself, grad_fother, grad_fnode = level_backward(latents, fine_self, fine_other, fine_node, own_term, table, summed, fine_n, fine_m, fine_lo, fine_hi, grad_updated.reshape(groups, parts, fine_rows, features))
    grad_weights = jnp.stack([grad_fself, grad_fother, grad_fnode, grad_cself, grad_cother, grad_cnode, grad_prolong])
    return result, grad_latent.astype(jnp.bfloat16), grad_weights
```

```python
import functools

import jax
import jax.numpy as jnp
from jax import lax
from jax.experimental import pallas as pl
from jax.experimental.pallas import tpu as pltpu
from jax.sharding import PartitionSpec as P

MESH = pl.DeviceIdType.MESH
BF = jnp.bfloat16
F32 = jnp.float32
D = 128
BLK = 64
TILE = 512


def dot(a, b, ca=1, cb=0):
    return lax.dot_general(a, b, (((ca,), (cb,)), ((), ())), preferred_element_type=F32)


def rows_at(start, size):
    return pl.ds(pl.multiple_of(start, size if size % 8 == 0 else 8), size)


def spread(row, rows):
    one = jnp.broadcast_to(row, (16, row.shape[1])).astype(BF)
    return jnp.concatenate([one] * (rows // 16), axis=0)


def iota_bf(rows, lanes, base=0):
    return (lax.broadcasted_iota(jnp.int32, (rows, lanes), 0) + base).astype(F32).astype(BF)


def one_hot(row, rows, base=0):
    hit = iota_bf(rows, row.shape[1], base) == spread(row, rows)
    return jnp.where(hit, jnp.ones((), BF), jnp.zeros((), BF))


def group_hot(values, group):
    inside = jnp.where((values >> 8) == group, values & 255, -1).astype(F32)
    return one_hot(inside, 256)


def prepare_slots(nbr, msk, cidx, rows, halo, halo_blocks):
    def body(p, carry):
        v = nbr[:, rows_at(p * 128, 128)]
        used = msk[:, rows_at(p * 128, 128)] > 0
        lane = lax.broadcasted_iota(jnp.int32, (8, 128), 1)
        slot = lax.broadcasted_iota(jnp.int32, (8, 128), 0)
        blk = 2 * p + (lane >> 6)
        hblk = blk & (halo_blocks - 1)
        col = jnp.where(
            v < rows,
            v - blk * BLK,
            jnp.where(v < rows + halo, v - rows - hblk * BLK + BLK, v - rows - halo - hblk * BLK + 2 * BLK),
        )
        col = jnp.where(used, col, -1)
        own = jnp.where(used, 3 * BLK + (lane & (BLK - 1)), -1)
        first = lane < BLK

        def halves(x):
            later = pltpu.roll(x, 4, 0)
            return (
                jnp.where(first, x, pltpu.roll(later, BLK, 1)),
                jnp.where(first, pltpu.roll(x, BLK, 1), later),
            )

        for half, (c, o) in enumerate(zip(halves(col), halves(own))):
            cidx[2 * p + half] = jnp.where(slot < 4, c, pltpu.roll(o, 4, 0)).astype(F32)
        return carry

    lax.fori_loop(0, rows // 128, body, 0)


def build_selectors(cidx, sel, blocks):
    def body(b, carry):
        idx = cidx[b]
        for j in range(4):
            sel[b, 0 : 3 * BLK, j * 128 : (j + 1) * 128] = one_hot(idx[j : j + 1], 3 * BLK)
            sel[b, 3 * BLK : 4 * BLK, j * 128 : (j + 1) * 128] = one_hot(idx[4 + j : 5 + j], BLK, 3 * BLK)
        return carry

    lax.fori_loop(0, blocks, body, 0)


def gather_rows(index, source, staged, start, count):
    def body(i, carry):
        at = pl.multiple_of(start + i * 16, 16)
        for u in range(16):
            staged[pl.ds(at + u, 1), :] = source[pl.ds(index[i * 16 + u], 1), :]
        return carry

    lax.fori_loop(0, count // 16, body, 0)


def edge_forward(sel, window):
    half = dot(sel, window, 0, 0)
    up = 1.0 + jnp.tanh(half)
    act = half * up
    slope = (up + act * (2.0 - up)).astype(BF)
    total = act[0:BLK]
    for k in range(1, 8):
        total = total + act[k * BLK : (k + 1) * BLK]
    return total, slope


def edge_backward(sel, slope, half_grad):
    grad = jnp.concatenate([half_grad] * 8, axis=0) * slope
    return dot(sel, grad)


def kernel(
    n_grp, n_sub,
    h, g, wfs, wfo, wfn, wcs, wco, wcn, wpr, nbr, msk, cnbr, cmsk,
    slo_s, shi_s, cslo_s, cshi_s, slo_v, shi_v, cslo_v, cshi_v, owner,
    result, grad_h, grad_w,
    stage, halo_in, halo, far, farh, own, cidx, sel, slope, st, summed, upd, gw, acc,
    hist, hist_in, rcnt, gsend, grs, gall, tsend, trs, cin, cinf, cstaged, cstage, chalo_in, chalo, cown, cfar, cfarh,
    ccidx, csel, yc, dsc, csum, cdown, cdfar, chacc, cback, cback_in, cout, cprol, mm, dsum, down, dfar, hacc, back, back_in,
    w_e, rs_e, ge_in, all_e, w_f, rs_f, gf_in, all_f,
    halo_ss, halo_rs, hist_ss, hist_rs, grs_ss, grs_rs, gag_ss, gag_rs, trs_ss, trs_rs, tag_ss, tag_rs,
    ch_ss, ch_rs, cb_ss, cb_rs, bk_ss, bk_rs, e_ss, e_rs, eg_ss, eg_rs, ea_ss, ea_rs, f_ss, f_rs, fg_ss, fg_rs, fa_ss, fa_rs,
):
    rows = h.shape[0]
    crows = cnbr.shape[1]
    halo_rows = shi_s.shape[0]
    chalo_rows = cshi_s.shape[0]
    tiles = rows // TILE
    blocks = rows // BLK
    cblocks = crows // BLK
    hblocks = halo_rows // BLK
    quarter = crows // n_grp
    gi = lax.axis_index("grp")
    si = lax.axis_index("sub")
    above = lax.rem(si + 1, n_sub)
    below = lax.rem(si + n_sub - 1, n_sub)
    has_below = jnp.where(si > 0, 1.0, 0.0).astype(F32)
    has_above = jnp.where(si < n_sub - 1, 1.0, 0.0).astype(F32)

    def to_sub(src, dst, ss, rs, there):
        return pltpu.make_async_remote_copy(
            src_ref=src, dst_ref=dst, send_sem=ss, recv_sem=rs, device_id={"sub": there}, device_id_type=MESH
        )

    def to_grp(src, dst, ss, rs, there):
        return pltpu.make_async_remote_copy(
            src_ref=src, dst_ref=dst, send_sem=ss, recv_sem=rs, device_id={"grp": there}, device_id_type=MESH
        )

    barrier = pltpu.get_barrier_semaphore()

    def greet(d, carry):
        pl.semaphore_signal(barrier, inc=1, device_id={"sub": lax.rem(si + d, n_sub)}, device_id_type=MESH)
        return carry

    lax.fori_loop(1, n_sub, greet, 0)
    for d in range(1, n_grp):
        pl.semaphore_signal(barrier, inc=1, device_id={"grp": lax.rem(gi + d, n_grp)}, device_id_type=MESH)

    def widen(i, carry):
        upd[rows_at(i * TILE, TILE), :] = h[rows_at(i * TILE, TILE), :].astype(F32)
        return carry

    lax.fori_loop(0, tiles, widen, 0)
    gather_rows(shi_s, upd, gw, 0, halo_rows)
    gather_rows(slo_s, upd, gw, halo_rows, halo_rows)
    stage[...] = gw[0 : 2 * halo_rows, :].astype(BF)
    pl.semaphore_wait(barrier, n_sub - 1 + n_grp - 1)
    half = halo_rows // 2
    halo_copies = []
    for c in range(4):
        part = pl.ds(c * half, half)
        halo_copies.append(
            to_sub(stage.at[part], halo_in.at[part], halo_ss.at[c], halo_rs.at[c], above if c < 2 else below)
        )
        halo_copies[-1].start()

    acc[...] = jnp.zeros_like(acc)
    hist[...] = jnp.zeros_like(hist)

    def owners(i, carry):
        high, low = [], []
        for l in range(TILE // 128):
            v = owner[pl.ds(i * (TILE // 128) + l, 1), :]
            for t in range(crows // 256):
                st[i, t * 256 : (t + 1) * 256, l * 128 : (l + 1) * 128] = group_hot(v, t)
            high.append(one_hot((v >> 7).astype(F32), 16))
            low.append(one_hot((v & 127).astype(F32), 128))
        hist[...] += dot(jnp.concatenate(high, axis=1), jnp.concatenate(low, axis=1), 1, 1)
        acc[...] += dot(st[i], g[rows_at(i * TILE, TILE), :])
        return carry

    lax.fori_loop(0, tiles, owners, 0)
    hist_copies = []
    for d in range(1, n_grp):
        hist_copies.append(
            to_grp(hist, hist_in.at[d - 1], hist_ss.at[d - 1], hist_rs.at[d - 1], lax.rem(gi + d, n_grp))
        )
        hist_copies[-1].start()

    def scatter_sum(sums, send, received, ss, rs):
        copies = []
        send[...] = sums[...].astype(BF)
        for d in range(1, n_grp):
            there = lax.rem(gi + d, n_grp)
            copies.append(
                to_grp(send.at[rows_at(there * quarter, quarter)], received.at[d - 1], ss.at[d - 1], rs.at[d - 1], there)
            )
            copies[-1].start()
        return copies

    def gather_all(array, ss, rs):
        copies = []
        mine = rows_at(gi * quarter, quarter)
        for d in range(1, n_grp):
            copies.append(
                to_grp(array.at[mine], array.at[mine], ss.at[d - 1], rs.at[d - 1], lax.rem(gi + d, n_grp))
            )
            copies[-1].start()
        return copies

    def my_sum(sums, received, copies):
        for c in copies:
            c.wait_recv()
        total = sums[rows_at(gi * quarter, quarter), :]
        for d in range(1, n_grp):
            total = total + received[d - 1].astype(F32)
        return total

    grs_copies = scatter_sum(acc, gsend, grs, grs_ss, grs_rs)

    prepare_slots(nbr, msk, cidx, rows, halo_rows, hblocks)
    prepare_slots(cnbr, cmsk, ccidx, crows, chalo_rows, 1)
    both_f = jnp.concatenate([wfs[...] * 0.5, wfo[...] * 0.5], axis=1)

    def dense(i, carry):
        part = rows_at(i * TILE, TILE)
        r = dot(h[part, :], both_f)
        own[part, :] = r[:, :D].astype(BF)
        far[part, :] = r[:, D:].astype(BF)
        gw[part, :] = dot(g[part, :], wfn[...], 1, 1) * 0.5
        return carry

    lax.fori_loop(0, tiles, dense, 0)
    build_selectors(cidx, sel, blocks)

    for c in hist_copies:
        c.wait_recv()
    counts = hist[...]
    for d in range(1, n_grp):
        counts = counts + hist_in[d - 1]
    for k in range(crows // 128):
        rcnt[k * 128 : (k + 1) * 128, :] = 1.0 / jnp.maximum(
            jnp.transpose(jnp.broadcast_to(counts[k : k + 1], (128, 128))), 1.0
        )
    gall[rows_at(gi * quarter, quarter), :] = my_sum(acc, grs, grs_copies).astype(BF)
    gag_copies = gather_all(gall, gag_ss, gag_rs)
    build_selectors(ccidx, csel, cblocks)

    for c in halo_copies:
        c.wait_recv()
    halo[0:halo_rows, :] = (halo_in[0:halo_rows, :].astype(F32) * has_below).astype(BF)
    halo[halo_rows:, :] = (halo_in[halo_rows:, :].astype(F32) * has_above).astype(BF)
    farh[...] = dot(halo[...], wfo[...] * 0.5).astype(BF)

    acc[...] = jnp.zeros_like(acc)

    def forward_tile(i, carry):
        def pair(p, carry):
            for u in range(2):
                b = i * (TILE // BLK) + p * 2 + u
                hb = b & (hblocks - 1)
                window = jnp.concatenate(
                    [
                        far[rows_at(b * BLK, BLK), :],
                        farh[rows_at(hb * BLK, BLK), :],
                        farh[rows_at(halo_rows + hb * BLK, BLK), :],
                        own[rows_at(b * BLK, BLK), :],
                    ],
                    axis=0,
                )
                total, q = edge_forward(sel[b], window)
                slope[b] = q
                summed[rows_at(b * BLK, BLK), :] = total.astype(BF)
            return carry

        lax.fori_loop(0, TILE // BLK // 2, pair, 0)
        part = rows_at(i * TILE, TILE)
        new = h[part, :].astype(F32) + dot(summed[part, :], wfn[...])
        upd[part, :] = new
        acc[...] += dot(st[i], new.astype(BF))
        return carry

    lax.fori_loop(0, tiles, forward_tile, 0)

    trs_copies = scatter_sum(acc, tsend, trs, trs_ss, trs_rs)
    for c in gag_copies:
        c.wait_recv()
    yc[...] = dot(gall[...], wpr[...], 1, 1)
    dsc[...] = (dot(yc[...].astype(BF), wcn[...], 1, 1) * 0.5).astype(BF)
    mine = rows_at(gi * quarter, quarter)
    cin[mine, :] = (my_sum(acc, trs, trs_copies) * rcnt[mine, :]).astype(BF)
    tag_copies = gather_all(cin, tag_ss, tag_rs)
    for c in tag_copies:
        c.wait_recv()

    cinf[...] = cin[...].astype(F32)
    gather_rows(cshi_s, cinf, cstaged, 0, chalo_rows)
    gather_rows(cslo_s, cinf, cstaged, chalo_rows, chalo_rows)
    cstage[...] = cstaged[...].astype(BF)
    ch_copies = []
    for c in range(2):
        part = pl.ds(c * chalo_rows, chalo_rows)
        ch_copies.append(to_sub(cstage.at[part], chalo_in.at[part], ch_ss.at[c], ch_rs.at[c], (above, below)[c]))
        ch_copies[-1].start()
    r = dot(cin[...], jnp.concatenate([wcs[...] * 0.5, wco[...] * 0.5], axis=1))
    cown[...] = r[:, :D].astype(BF)
    cfar[...] = r[:, D:].astype(BF)
    for c in ch_copies:
        c.wait_recv()
    chalo[0:chalo_rows, :] = (chalo_in[0:chalo_rows, :].astype(F32) * has_below).astype(BF)
    chalo[chalo_rows:, :] = (chalo_in[chalo_rows:, :].astype(F32) * has_above).astype(BF)
    cfarh[...] = dot(chalo[...], wco[...] * 0.5).astype(BF)
    chacc[...] = jnp.zeros_like(chacc)

    def mid_pair(p, carry):
        for u in range(2):
            b = p * 2 + u
            part = rows_at(b * BLK, BLK)
            total, q = edge_forward(csel[b], jnp.concatenate([cfar[part, :], cfarh[...], cown[part, :]], axis=0))
            csum[part, :] = total.astype(BF)
            grads = edge_backward(csel[b], q, dsc[part, :])
            cdfar[part, :] = grads[0:BLK]
            chacc[...] += grads[BLK : 3 * BLK]
            cdown[part, :] = grads[3 * BLK :].astype(BF)
        return carry

    lax.fori_loop(0, cblocks // 2, mid_pair, 0)
    cback[...] = chacc[...].astype(BF)
    cb_copies = []
    for c in range(2):
        part = pl.ds(c * chalo_rows, chalo_rows)
        cb_copies.append(to_sub(cback.at[part], cback_in.at[part], cb_ss.at[c], cb_rs.at[c], (below, above)[c]))
        cb_copies[-1].start()

    cout[...] = (cin[...].astype(F32) + dot(csum[...], wcn[...])).astype(BF)
    cprol[...] = dot(cout[...], wpr[...]).astype(BF)
    shared = 1.0 / n_grp
    w_e[128:256, :] = dot(cin[...], cdown[...], 0, 0) * shared
    w_e[256:384, :] = (dot(cin[...], cdfar[...].astype(BF), 0, 0) + dot(chalo[...], cback[...], 0, 0)) * shared
    w_e[384:512, :] = dot(csum[...], yc[...].astype(BF), 0, 0) * shared
    w_e[512:640, :] = dot(cout[...], gall[...], 0, 0) * shared
    w_e[640:768, :] = jnp.zeros((128, 128), F32)

    def prolonged(i, carry):
        part = rows_at(i * TILE, TILE)
        result[part, :] = (upd[part, :] + dot(st[i], cprol[...], 0, 0)).astype(BF)
        return carry

    lax.fori_loop(0, tiles, prolonged, 0)
    for c in cb_copies:
        c.wait_recv()
    from_above = (cback_in[0:chalo_rows, :].astype(F32) * has_above).astype(BF)
    from_below = (cback_in[chalo_rows:, :].astype(F32) * has_below).astype(BF)
    for t in range(crows // 256):
        part = slice(t * 256, (t + 1) * 256)
        cdfar[part, :] += dot(group_hot(cshi_v[...], t), from_above) + dot(group_hot(cslo_v[...], t), from_below)
    dcin = yc[...] + dot(cdown[...], wcs[...], 1, 1) + dot(cdfar[...].astype(BF), wco[...], 1, 1)
    m = (dcin * rcnt[...]).astype(BF)
    mm[:, :D] = m
    mm[:, D:] = (dot(m, wfn[...], 1, 1) * 0.5).astype(BF)

    w_e[0:128, :] = jnp.zeros((128, 128), F32)

    def cotangents(i, carry):
        part = rows_at(i * TILE, TILE)
        r = dot(st[i], mm[...], 0, 0)
        y = g[part, :].astype(F32) + r[:, :D]
        upd[part, :] = y
        dsum[part, :] = (gw[part, :] + r[:, D:]).astype(BF)
        w_e[0:128, :] += dot(summed[part, :], y.astype(BF), 0, 0)
        return carry

    lax.fori_loop(0, tiles, cotangents, 0)

    def weights_scatter(array, received, ss, rs):
        size = array.shape[0] // n_sub

        def body(d, carry):
            there = lax.rem(si + d, n_sub)
            to_sub(array.at[rows_at(there * size, size)], received.at[rows_at((d - 1) * size, size)], ss, rs, there).start()
            return carry

        lax.fori_loop(1, n_sub, body, 0)

    def weights_group(array, received, group_in, ss, rs, gss, grs_):
        size = array.shape[0] // n_sub
        to_sub(received, received, ss, rs, above).wait_recv()

        def body(d, total):
            return total + received[rows_at((d - 1) * size, size), :]

        group_in[gi] = lax.fori_loop(1, n_sub, body, array[rows_at(si * size, size), :])
        copies = []
        for d in range(1, n_grp):
            copies.append(to_grp(group_in.at[gi], group_in.at[gi], gss.at[d - 1], grs_.at[d - 1], lax.rem(gi + d, n_grp)))
            copies[-1].start()
        return copies

    def weights_gather(array, group_in, copies, ss, rs):
        size = array.shape[0] // n_sub
        for c in copies:
            c.wait_recv()
        total = group_in[0]
        for k in range(1, n_grp):
            total = total + group_in[k]
        mine = rows_at(si * size, size)
        array[mine, :] = total

        def body(d, carry):
            to_sub(array.at[mine], array.at[mine], ss, rs, lax.rem(si + d, n_sub)).start()
            return carry

        lax.fori_loop(1, n_sub, body, 0)

    weights_scatter(w_e, rs_e, e_ss, e_rs)

    bk_copies = []
    for c in range(2 * hblocks):
        part = pl.ds(c * BLK, BLK)
        bk_copies.append(
            to_sub(back.at[part], back_in.at[part], bk_ss.at[c], bk_rs.at[c], below if c < hblocks else above)
        )

    def backward_halo_block(hb, carry):
        hacc[...] = jnp.zeros_like(hacc)

        def pair(p, carry):
            both = None
            for u in range(2):
                b = (p * 2 + u) * hblocks + hb
                part = rows_at(b * BLK, BLK)
                grads = edge_backward(sel[b], slope[b], dsum[part, :])
                dfar[part, :] = grads[0:BLK].astype(BF)
                down[part, :] = grads[3 * BLK :].astype(BF)
                both = grads[BLK : 3 * BLK] if both is None else both + grads[BLK : 3 * BLK]
            hacc[...] += both
            return carry

        lax.fori_loop(0, blocks // hblocks // 2, pair, 0)
        back[rows_at(hb * BLK, BLK), :] = hacc[0:BLK, :].astype(BF)
        back[rows_at(halo_rows + hb * BLK, BLK), :] = hacc[BLK:, :].astype(BF)
        for c, there in ((hb, below), (hblocks + hb, above)):
            part = rows_at(c * BLK, BLK)
            to_sub(back.at[part], back_in.at[part], bk_ss.at[c], bk_rs.at[c], there).start()
        return carry

    lax.fori_loop(0, hblocks // 2, backward_halo_block, 0)
    eg_copies = weights_group(w_e, rs_e, ge_in, e_ss, e_rs, eg_ss, eg_rs)
    lax.fori_loop(hblocks // 2, hblocks, backward_halo_block, 0)
    weights_gather(all_e, ge_in, eg_copies, ea_ss, ea_rs)

    w_f[0:128, :] = jnp.zeros((128, 128), F32)
    w_f[128:256, :] = dot(halo[...], back[...], 0, 0)

    def last_weights(i, carry):
        part = rows_at(i * TILE, TILE)
        r = dot(h[part, :], jnp.concatenate([down[part, :], dfar[part, :]], axis=1), 0, 0)
        w_f[0:128, :] += r[:, :D]
        w_f[128:256, :] += r[:, D:]
        return carry

    lax.fori_loop(0, tiles, last_weights, 0)
    weights_scatter(w_f, rs_f, f_ss, f_rs)

    def latent_part(i, carry):
        part = rows_at(i * TILE, TILE)
        upd[part, :] += dot(down[part, :], wfs[...], 1, 1) + dot(dfar[part, :], wfo[...], 1, 1)
        return carry

    lax.fori_loop(0, tiles, latent_part, 0)
    fg_copies = weights_group(w_f, rs_f, gf_in, f_ss, f_rs, fg_ss, fg_rs)

    for c in bk_copies:
        c.wait_recv()
    halo[0:halo_rows, :] = (dot(back_in[0:halo_rows, :], wfo[...], 1, 1) * has_above).astype(BF)
    halo[halo_rows:, :] = (dot(back_in[halo_rows:, :], wfo[...], 1, 1) * has_below).astype(BF)
    group = 1024

    def returned(i, carry):
        part = rows_at(i * group, group)
        hots = []
        for t in range(group // 256):
            row = []
            for table in (shi_v, slo_v):
                for l in range(halo_rows // 128):
                    row.append(group_hot(table[l : l + 1, :], i * (group // 256) + t))
            hots.append(jnp.concatenate(row, axis=1))
        grad_h[part, :] = (upd[part, :] + dot(jnp.concatenate(hots, axis=0), halo[...])).astype(BF)
        return carry

    lax.fori_loop(0, rows // group // 2, returned, 0)
    weights_gather(all_f, gf_in, fg_copies, fa_ss, fa_rs)
    lax.fori_loop(rows // group // 2, rows // group, returned, 0)

    def finish(array, ss, rs, first, count):
        size = array.shape[0] // n_sub
        others = array.at[pl.ds(0, array.shape[0] - size)]
        to_sub(others, others, ss, rs, above).wait_recv()
        for k in range(count):
            grad_w[first + k] = array[k * 128 : (k + 1) * 128, :]

    finish(all_e, ea_ss, ea_rs, 2, 5)
    finish(all_f, fa_ss, fa_rs, 0, 2)

    for c in halo_copies + hist_copies + grs_copies + gag_copies + trs_copies + tag_copies + ch_copies + cb_copies:
        c.wait_send()
    for c in bk_copies + eg_copies + fg_copies:
        c.wait_send()
    for received, array, ss, gather_ss, rs in ((rs_e, all_e, e_ss, ea_ss, e_rs), (rs_f, all_f, f_ss, fa_ss, f_rs)):
        to_sub(received, received, ss, rs, above).wait_send()
        others = array.at[pl.ds(0, array.shape[0] - array.shape[0] // n_sub)]
        to_sub(others, others, gather_ss, rs, above).wait_send()


def step(
    n_grp, n_sub,
    states, cotangent, fine_self, fine_other, fine_node, coarse_self, coarse_other, coarse_node, prolong,
    fine_nbr, fine_mask, fine_send_lo, fine_send_hi, coarse_nbr, coarse_mask, coarse_send_lo, coarse_send_hi, coarse_owner,
):
    rows, slots = fine_nbr.shape
    crows = coarse_nbr.shape[0]
    halo = fine_send_lo.shape[0]
    chalo = coarse_send_lo.shape[0]
    blocks, cblocks = rows // BLK, crows // BLK
    edges = BLK * slots
    quarter = crows // n_grp
    vmem = pl.BlockSpec(memory_space=pltpu.VMEM)
    smem = pl.BlockSpec(memory_space=pltpu.SMEM)
    V = pltpu.VMEM
    dma = pltpu.SemaphoreType.DMA
    e_rows, f_rows = 768, 256
    ce, cf = e_rows // n_sub, f_rows // n_sub
    scratch = [
        V((2 * halo, D), BF), V((2 * halo, D), BF), V((2 * halo, D), BF),
        V((rows, D), BF), V((2 * halo, D), BF), V((rows, D), BF),
        V((blocks, 8, 128), F32), V((blocks, 4 * BLK, edges), BF), V((blocks, edges, D), BF),
        V((rows // TILE, crows, TILE), BF),
        V((rows, D), BF), V((rows, D), F32), V((rows, D), F32), V((crows, D), F32),
        V((16, 128), F32), V((n_grp - 1, 16, 128), F32), V((crows, D), F32),
        V((crows, D), BF), V((n_grp - 1, quarter, D), BF), V((crows, D), BF),
        V((crows, D), BF), V((n_grp - 1, quarter, D), BF), V((crows, D), BF),
        V((crows, D), F32), V((2 * chalo, D), F32), V((2 * chalo, D), BF), V((2 * chalo, D), BF), V((2 * chalo, D), BF),
        V((crows, D), BF), V((crows, D), BF), V((2 * chalo, D), BF),
        V((cblocks, 8, 128), F32), V((cblocks, 4 * BLK, edges), BF),
        V((crows, D), F32), V((crows, D), BF), V((crows, D), BF), V((crows, D), BF), V((crows, D), F32),
        V((2 * chalo, D), F32), V((2 * chalo, D), BF), V((2 * chalo, D), BF),
        V((crows, D), BF), V((crows, D), BF), V((crows, 2 * D), BF),
        V((rows, D), BF), V((rows, D), BF), V((rows, D), BF),
        V((2 * BLK, D), F32), V((2 * halo, D), BF), V((2 * halo, D), BF),
        V((e_rows, D), F32), V((e_rows - ce, D), F32), V((n_grp, ce, D), F32), V((e_rows, D), F32),
        V((f_rows, D), F32), V((f_rows - cf, D), F32), V((n_grp, cf, D), F32), V((f_rows, D), F32),
        dma((4,)), dma((4,)),
        dma((n_grp - 1,)), dma((n_grp - 1,)), dma((n_grp - 1,)), dma((n_grp - 1,)), dma((n_grp - 1,)), dma((n_grp - 1,)),
        dma((n_grp - 1,)), dma((n_grp - 1,)), dma((n_grp - 1,)), dma((n_grp - 1,)),
        dma((2,)), dma((2,)), dma((2,)), dma((2,)),
        dma((2 * halo // BLK,)), dma((2 * halo // BLK,)),
        dma, dma, dma((n_grp - 1,)), dma((n_grp - 1,)), dma, dma,
        dma, dma, dma((n_grp - 1,)), dma((n_grp - 1,)), dma, dma,
    ]
    return pl.pallas_call(
        functools.partial(kernel, n_grp, n_sub),
        out_shape=(
            jax.ShapeDtypeStruct((rows, D), BF),
            jax.ShapeDtypeStruct((rows, D), BF),
            jax.ShapeDtypeStruct((7, D, D), F32),
        ),
        in_specs=[vmem] * 13 + [smem] * 4 + [vmem] * 5,
        out_specs=(vmem, vmem, vmem),
        scratch_shapes=scratch,
        compiler_params=pltpu.CompilerParams(
            collective_id=0, has_side_effects=True, vmem_limit_bytes=63 * 1024 * 1024
        ),
    )(
        states, cotangent, fine_self, fine_other, fine_node, coarse_self, coarse_other, coarse_node, prolong,
        fine_nbr.T, fine_mask.T, coarse_nbr.T, coarse_mask.T,
        fine_send_lo, fine_send_hi, coarse_send_lo, coarse_send_hi,
        fine_send_lo.reshape(-1, 128), fine_send_hi.reshape(-1, 128),
        coarse_send_lo.reshape(1, -1), coarse_send_hi.reshape(1, -1),
        coarse_owner.reshape(-1, 128),
    )


def solution(mesh):
    rows2 = P(("grp", "sub"), None)
    rows1 = P(("grp", "sub"))
    in_specs = (
        (rows2, rows2) + (P(),) * 7
        + (rows2, rows2, rows1, rows1)
        + (P("sub", None), P("sub", None), P("sub"), P("sub"), rows1)
    )
    return jax.shard_map(
        functools.partial(step, mesh.shape["grp"], mesh.shape["sub"]),
        mesh=mesh, in_specs=in_specs, out_specs=(rows2, rows2, P()), check_vma=False,
    )
```

```python
import functools

import jax
import jax.numpy as jnp
from jax import lax
from jax.experimental import pallas as pl
from jax.experimental.pallas import tpu as pltpu
from jax.sharding import PartitionSpec as P

MESH = pl.DeviceIdType.MESH
BF = jnp.bfloat16
F32 = jnp.float32
D = 128
BLK = 64
TILE = 512


def dot(a, b, ca=1, cb=0):
    return lax.dot_general(a, b, (((ca,), (cb,)), ((), ())), preferred_element_type=F32)


def rows_at(start, size):
    if isinstance(start, int):
        return pl.ds(start, size)
    return pl.ds(pl.multiple_of(start, size if size % 8 == 0 else 8), size)


def spread(row, rows):
    one = jnp.broadcast_to(row, (16, row.shape[1])).astype(BF)
    return jnp.concatenate([one] * (rows // 16), axis=0)


def iota_bf(rows, lanes, base=0):
    return (lax.broadcasted_iota(jnp.int32, (rows, lanes), 0) + base).astype(F32).astype(BF)


def one_hot(row, rows, base=0):
    hit = iota_bf(rows, row.shape[1], base) == spread(row, rows)
    return jnp.where(hit, jnp.ones((), BF), jnp.zeros((), BF))


def group_hot(values, group):
    inside = jnp.where((values >> 8) == group, values & 255, -1).astype(F32)
    return one_hot(inside, 256)


def prepare_slots(nbr, msk, cidx, rows, halo, halo_blocks):
    def body(p, carry):
        v = nbr[:, rows_at(p * 128, 128)]
        used = msk[:, rows_at(p * 128, 128)] > 0
        lane = lax.broadcasted_iota(jnp.int32, (8, 128), 1)
        slot = lax.broadcasted_iota(jnp.int32, (8, 128), 0)
        blk = 2 * p + (lane >> 6)
        hblk = blk & (halo_blocks - 1)
        col = jnp.where(
            v < rows,
            v - blk * BLK,
            jnp.where(v < rows + halo, v - rows - hblk * BLK + BLK, v - rows - halo - hblk * BLK + 2 * BLK),
        )
        col = jnp.where(used, col, -1)
        own = jnp.where(used, 3 * BLK + (lane & (BLK - 1)), -1)
        first = lane < BLK

        def halves(x):
            later = pltpu.roll(x, 4, 0)
            return (
                jnp.where(first, x, pltpu.roll(later, BLK, 1)),
                jnp.where(first, pltpu.roll(x, BLK, 1), later),
            )

        for half, (c, o) in enumerate(zip(halves(col), halves(own))):
            cidx[2 * p + half] = jnp.where(slot < 4, c, pltpu.roll(o, 4, 0)).astype(F32)
        return carry

    lax.fori_loop(0, rows // 128, body, 0)


def build_selectors(cidx, sel, blocks):
    def body(p, carry):
        for u in range(4):
            b = p * 4 + u
            idx = cidx[b]
            for j in range(4):
                sel[b, 0 : 3 * BLK, j * 128 : (j + 1) * 128] = one_hot(idx[j : j + 1], 3 * BLK)
                sel[b, 3 * BLK : 4 * BLK, j * 128 : (j + 1) * 128] = one_hot(idx[4 + j : 5 + j], BLK, 3 * BLK)
        return carry

    lax.fori_loop(0, blocks // 4, body, 0)


def gather_rows(index, source, staged, start, count):
    def body(i, carry):
        at = pl.multiple_of(start + i * 16, 16)
        for u in range(16):
            staged[pl.ds(at + u, 1), :] = source[pl.ds(index[i * 16 + u], 1), :]
        return carry

    lax.fori_loop(0, count // 16, body, 0)


def edge_forward(sel, window):
    half = dot(sel, window, 0, 0)
    up = 1.0 + jnp.tanh(half)
    act = half * up
    slope = (up + act * (2.0 - up)).astype(BF)
    total = act[0:BLK]
    for k in range(1, 8):
        total = total + act[k * BLK : (k + 1) * BLK]
    return total, slope


def edge_backward(sel, slope, half_grad):
    grad = jnp.concatenate([half_grad] * 8, axis=0) * slope
    return dot(sel, grad)


def kernel(
    n_grp, n_sub,
    h_hbm, g_hbm, wfs, wfo, wfn, wcs, wco, wcn, wpr, nbr_hbm, msk_hbm, cnbr_hbm, cmsk_hbm,
    slo_s, shi_s, cslo_s, cshi_s, slo_v, shi_v, cslo_v, cshi_v, owner,
    result_hbm, grad_h_hbm, grad_w,
    h, g, nbr, msk, cnbr, cmsk, result, grad_h,
    stage, halo_in, halo, far_dfar, farh, own_dsum, cidx, sel, slope, st, summed_down, upd, rowbuf, acc,
    hist, hist_in, rcnt, gsend, gcore, gchip, gx, gall, tsend, tcore, tchip, tx, cin, cinf, cstaged, cstage, chalo_in, chalo, cown, cfar, cfarh,
    ccidx, csel, yc, dsc, csum, cdown, cdfar, chacc, cback, cback_in, cout, cprol, mm, back, back_in,
    w_e, rs_e, all_e, w_f, sum_f, rs_f, grp_f, all_f,
    load_s, store_s, halo_ss, halo_rs, hist_ss, hist_rs, gs_ss, gs_rs, ts_ss, ts_rs,
    ch_ss, ch_rs, cb_ss, cb_rs, bk_ss, bk_rs, e_ss, e_rs, ea_ss, ea_rs, f_ss, f_rs, fg_ss, fg_rs, fa_ss, fa_rs,
):
    own, dsum = own_dsum, own_dsum
    far, dfar = far_dfar, far_dfar
    summed, down = summed_down, summed_down
    gw = rowbuf
    rows = h.shape[0]
    crows = cnbr.shape[1]
    halo_rows = shi_s.shape[0]
    chalo_rows = cshi_s.shape[0]
    tiles = rows // TILE
    blocks = rows // BLK
    cblocks = crows // BLK
    hblocks = halo_rows // BLK
    gi = lax.axis_index("grp")
    si = lax.axis_index("sub")
    above = lax.rem(si + 1, n_sub)
    below = lax.rem(si + n_sub - 1, n_sub)
    has_below = jnp.where(si > 0, 1.0, 0.0).astype(F32)
    has_above = jnp.where(si < n_sub - 1, 1.0, 0.0).astype(F32)

    def to_sub(src, dst, ss, rs, there):
        return pltpu.make_async_remote_copy(
            src_ref=src, dst_ref=dst, send_sem=ss, recv_sem=rs, device_id={"sub": there}, device_id_type=MESH
        )

    def to_grp(src, dst, ss, rs, there):
        return pltpu.make_async_remote_copy(
            src_ref=src, dst_ref=dst, send_sem=ss, recv_sem=rs, device_id={"grp": there}, device_id_type=MESH
        )

    loads = []
    for k, (src, dst) in enumerate(
        ((h_hbm, h), (g_hbm, g), (nbr_hbm, nbr), (msk_hbm, msk), (cnbr_hbm, cnbr), (cmsk_hbm, cmsk))
    ):
        loads.append(pltpu.make_async_copy(src, dst, load_s.at[k]))
        loads[-1].start()

    def weights_scatter(array, received, ss, rs):
        size = array.shape[0] // n_sub

        def body(d, carry):
            there = lax.rem(si + d, n_sub)
            to_sub(array.at[rows_at(there * size, size)], received.at[rows_at((d - 1) * size, size)], ss, rs, there).start()
            return carry

        lax.fori_loop(1, n_sub, body, 0)

    def weights_sum(array, received, ss, rs):
        size = array.shape[0] // n_sub
        to_sub(received, received, ss, rs, above).wait_recv()

        def body(d, total):
            return total + received[rows_at((d - 1) * size, size), :].astype(F32)

        return lax.fori_loop(1, n_sub, body, array[rows_at(si * size, size), :].astype(F32))

    def weights_gather(array, total, ss, rs):
        size = array.shape[0] // n_sub
        mine = rows_at(si * size, size)
        array[mine, :] = total.astype(BF)

        def body(d, carry):
            to_sub(array.at[mine], array.at[mine], ss, rs, lax.rem(si + d, n_sub)).start()
            return carry

        lax.fori_loop(1, n_sub, body, 0)

    barrier = pltpu.get_barrier_semaphore()

    def greet(d, carry):
        pl.semaphore_signal(barrier, inc=1, device_id={"sub": lax.rem(si + d, n_sub)}, device_id_type=MESH)
        return carry

    lax.fori_loop(1, n_sub, greet, 0)
    for d in range(1, n_grp):
        pl.semaphore_signal(barrier, inc=1, device_id={"grp": lax.rem(gi + d, n_grp)}, device_id_type=MESH)

    def widen(i, carry):
        upd[rows_at(i * TILE, TILE), :] = h[rows_at(i * TILE, TILE), :].astype(F32)
        return carry

    loads[0].wait()
    lax.fori_loop(0, tiles, widen, 0)
    gather_rows(shi_s, upd, rowbuf, 0, halo_rows)
    gather_rows(slo_s, upd, rowbuf, halo_rows, halo_rows)
    stage[...] = rowbuf[0 : 2 * halo_rows, :].astype(BF)
    pl.semaphore_wait(barrier, n_sub - 1 + n_grp - 1)
    half = halo_rows // 2
    halo_copies = []
    for c in range(4):
        part = pl.ds(c * half, half)
        halo_copies.append(
            to_sub(stage.at[part], halo_in.at[part], halo_ss.at[c], halo_rs.at[c], above if c < 2 else below)
        )
        halo_copies[-1].start()

    loads[1].wait()
    acc[...] = jnp.zeros_like(acc)
    hist[...] = jnp.zeros_like(hist)

    def owners(i, carry):
        high, low = [], []
        for l in range(TILE // 128):
            v = owner[pl.ds(i * (TILE // 128) + l, 1), :]
            for t in range(crows // 256):
                st[i, t * 256 : (t + 1) * 256, l * 128 : (l + 1) * 128] = group_hot(v, t)
            high.append(one_hot((v >> 7).astype(F32), 16))
            low.append(one_hot((v & 127).astype(F32), 128))
        hist[...] += dot(jnp.concatenate(high, axis=1), jnp.concatenate(low, axis=1), 1, 1)
        acc[...] += dot(st[i], g[rows_at(i * TILE, TILE), :])
        return carry

    lax.fori_loop(0, tiles, owners, 0)
    hist_copies = []
    for d in range(1, n_grp):
        hist_copies.append(
            to_grp(hist, hist_in.at[d - 1], hist_ss.at[d - 1], hist_rs.at[d - 1], lax.rem(gi + d, n_grp))
        )
        hist_copies[-1].start()

    core = lax.rem(gi, 2)
    sibling = gi + 1 - 2 * core
    other_chip = lax.rem(gi + 2, n_grp)
    part_rows = crows // 2
    mine = rows_at(core * part_rows, part_rows)
    theirs = rows_at((1 - core) * part_rows, part_rows)

    def group_first(sums, send, received, ss, rs):
        send[...] = sums[...].astype(BF)
        copy = to_grp(send.at[theirs], received, ss.at[0], rs.at[0], sibling)
        copy.start()
        return [copy]

    def group_second(copies, sums, received, chip, other, ss, rs):
        copies[0].wait_recv()
        chip[...] = (sums[mine, :] + received[...].astype(F32)).astype(BF)
        copies.append(to_grp(chip, other, ss.at[1], rs.at[1], other_chip))
        copies[1].start()

    def group_third(copies, chip, other, scale, whole, ss, rs):
        copies[1].wait_recv()
        total = chip[...].astype(F32) + other[...].astype(F32)
        whole[mine, :] = (total if scale is None else total * scale[mine, :]).astype(BF)
        copies.append(to_grp(whole.at[mine], whole.at[mine], ss.at[2], rs.at[2], sibling))
        copies[2].start()

    g_copies = group_first(acc, gsend, gcore, gs_ss, gs_rs)

    for c in loads[2:]:
        c.wait()
    prepare_slots(nbr, msk, cidx, rows, halo_rows, hblocks)
    both_f = jnp.concatenate([wfs[...] * 0.5, wfo[...] * 0.5], axis=1)

    def dense(i, carry):
        part = rows_at(i * TILE, TILE)
        r = dot(h[part, :], both_f)
        own[part, :] = r[:, :D].astype(BF)
        far[part, :] = r[:, D:].astype(BF)
        return carry

    lax.fori_loop(0, tiles, dense, 0)
    build_selectors(cidx, sel, blocks)

    group_second(g_copies, acc, gcore, gchip, gx, gs_ss, gs_rs)

    for c in halo_copies:
        c.wait_recv()
    halo[0:halo_rows, :] = (halo_in[0:halo_rows, :].astype(F32) * has_below).astype(BF)
    halo[halo_rows:, :] = (halo_in[halo_rows:, :].astype(F32) * has_above).astype(BF)
    farh[...] = dot(halo[...], wfo[...] * 0.5).astype(BF)

    acc[...] = jnp.zeros_like(acc)

    def forward_edges(i):
        for u in range(TILE // BLK):
            b = i * (TILE // BLK) + u
            hb = b & (hblocks - 1)
            window = jnp.concatenate(
                [
                    far[rows_at(b * BLK, BLK), :],
                    farh[rows_at(hb * BLK, BLK), :],
                    farh[rows_at(halo_rows + hb * BLK, BLK), :],
                    own[rows_at(b * BLK, BLK), :],
                ],
                axis=0,
            )
            total, q = edge_forward(sel[b], window)
            slope[b] = q
            summed[rows_at(b * BLK, BLK), :] = total.astype(BF)

    def forward_update(i):
        part = rows_at(i * TILE, TILE)
        new = h[part, :].astype(F32) + dot(summed[part, :], wfn[...])
        upd[part, :] = new
        acc[...] += dot(st[i], new.astype(BF))

    def forward_tiles(p, carry):
        forward_update(p * 2 - 2)
        forward_update(p * 2 - 1)
        forward_edges(p * 2)
        forward_edges(p * 2 + 1)
        return carry

    forward_edges(0)
    forward_edges(1)
    lax.fori_loop(1, tiles // 2, forward_tiles, 0)
    forward_update(tiles - 2)
    forward_update(tiles - 1)

    group_third(g_copies, gchip, gx, None, gall, gs_ss, gs_rs)
    t_copies = group_first(acc, tsend, tcore, ts_ss, ts_rs)
    for c in hist_copies:
        c.wait_recv()
    counts = hist[...]
    for d in range(1, n_grp):
        counts = counts + hist_in[d - 1]
    for k in range(crows // 128):
        rcnt[k * 128 : (k + 1) * 128, :] = 1.0 / jnp.maximum(
            jnp.transpose(jnp.broadcast_to(counts[k : k + 1], (128, 128))), 1.0
        )
    prepare_slots(cnbr, cmsk, ccidx, crows, chalo_rows, 1)
    g_copies[2].wait_recv()
    yc[...] = dot(gall[...], wpr[...], 1, 1)
    group_second(t_copies, acc, tcore, tchip, tx, ts_ss, ts_rs)
    dsc[...] = (dot(yc[...].astype(BF), wcn[...], 1, 1) * 0.5).astype(BF)
    build_selectors(ccidx, csel, cblocks)
    group_third(t_copies, tchip, tx, rcnt, cin, ts_ss, ts_rs)
    t_copies[2].wait_recv()

    cinf[...] = cin[...].astype(F32)
    gather_rows(cshi_s, cinf, cstaged, 0, chalo_rows)
    gather_rows(cslo_s, cinf, cstaged, chalo_rows, chalo_rows)
    cstage[...] = cstaged[...].astype(BF)
    ch_copies = []
    for c in range(2):
        part = pl.ds(c * chalo_rows, chalo_rows)
        ch_copies.append(to_sub(cstage.at[part], chalo_in.at[part], ch_ss.at[c], ch_rs.at[c], (above, below)[c]))
        ch_copies[-1].start()
    r = dot(cin[...], jnp.concatenate([wcs[...] * 0.5, wco[...] * 0.5], axis=1))
    cown[...] = r[:, :D].astype(BF)
    cfar[...] = r[:, D:].astype(BF)

    def known_part(i, carry):
        part = rows_at(i * TILE, TILE)
        gw[part, :] = dot(g[part, :], wfn[...], 1, 1) * 0.5
        return carry

    lax.fori_loop(0, tiles, known_part, 0)
    for c in ch_copies:
        c.wait_recv()
    chalo[0:chalo_rows, :] = (chalo_in[0:chalo_rows, :].astype(F32) * has_below).astype(BF)
    chalo[chalo_rows:, :] = (chalo_in[chalo_rows:, :].astype(F32) * has_above).astype(BF)
    cfarh[...] = dot(chalo[...], wco[...] * 0.5).astype(BF)
    chacc[...] = jnp.zeros_like(chacc)

    def mid_blocks(p, carry):
        both = None
        for u in range(8):
            b = p * 8 + u
            part = rows_at(b * BLK, BLK)
            total, q = edge_forward(csel[b], jnp.concatenate([cfar[part, :], cfarh[...], cown[part, :]], axis=0))
            csum[part, :] = total.astype(BF)
            grads = edge_backward(csel[b], q, dsc[part, :])
            cdfar[part, :] = grads[0:BLK]
            both = grads[BLK : 3 * BLK] if both is None else both + grads[BLK : 3 * BLK]
            cdown[part, :] = grads[3 * BLK :].astype(BF)
        chacc[...] += both
        return carry

    lax.fori_loop(0, cblocks // 8, mid_blocks, 0)
    cback[...] = chacc[...].astype(BF)
    cb_copies = []
    for c in range(2):
        part = pl.ds(c * chalo_rows, chalo_rows)
        cb_copies.append(to_sub(cback.at[part], cback_in.at[part], cb_ss.at[c], cb_rs.at[c], (below, above)[c]))
        cb_copies[-1].start()

    cout[...] = (cin[...].astype(F32) + dot(csum[...], wcn[...])).astype(BF)
    cprol[...] = dot(cout[...], wpr[...]).astype(BF)
    w_e[0:128, :] = dot(cin[...], cdown[...], 0, 0).astype(BF)
    w_e[128:256, :] = (dot(cin[...], cdfar[...].astype(BF), 0, 0) + dot(chalo[...], cback[...], 0, 0)).astype(BF)
    w_e[256:384, :] = dot(csum[...], yc[...].astype(BF), 0, 0).astype(BF)
    w_e[384:512, :] = dot(cout[...], gall[...], 0, 0).astype(BF)
    weights_scatter(w_e, rs_e, e_ss, e_rs)

    def prolonged(p, carry):
        for u in range(2):
            i = p * 2 + u
            part = rows_at(i * TILE, TILE)
            result[part, :] = (upd[part, :] + dot(st[i], cprol[...], 0, 0)).astype(BF)
        return carry

    lax.fori_loop(0, tiles // 2, prolonged, 0)
    stores = [pltpu.make_async_copy(result, result_hbm, store_s.at[0])]
    stores[0].start()
    for c in cb_copies:
        c.wait_recv()
    from_above = (cback_in[0:chalo_rows, :].astype(F32) * has_above).astype(BF)
    from_below = (cback_in[chalo_rows:, :].astype(F32) * has_below).astype(BF)
    for t in range(crows // 256):
        part = slice(t * 256, (t + 1) * 256)
        cdfar[part, :] += dot(group_hot(cshi_v[...], t), from_above) + dot(group_hot(cslo_v[...], t), from_below)
    dcin = yc[...] + dot(cdown[...], wcs[...], 1, 1) + dot(cdfar[...].astype(BF), wco[...], 1, 1)
    m = (dcin * rcnt[...]).astype(BF)
    mm[:, :D] = m
    mm[:, D:] = (dot(m, wfn[...], 1, 1) * 0.5).astype(BF)
    weights_gather(all_e, weights_sum(w_e, rs_e, e_ss, e_rs), ea_ss, ea_rs)

    sum_f[...] = jnp.zeros_like(sum_f)

    def cotangents(p, carry):
        for u in range(2):
            i = p * 2 + u
            part = rows_at(i * TILE, TILE)
            r = dot(st[i], mm[...], 0, 0)
            y = g[part, :].astype(F32) + r[:, :D]
            upd[part, :] = y
            dsum[part, :] = (gw[part, :] + r[:, D:]).astype(BF)
            sum_f[256:384, :] += dot(summed[part, :], y.astype(BF), 0, 0)
        return carry

    lax.fori_loop(0, tiles // 2, cotangents, 0)

    bk_copies = []
    for c in range(2 * hblocks):
        part = pl.ds(c * BLK, BLK)
        bk_copies.append(
            to_sub(back.at[part], back_in.at[part], bk_ss.at[c], bk_rs.at[c], below if c < hblocks else above)
        )

    def backward_edges(hb):
        both = None
        for u in range(blocks // hblocks):
            b = u * hblocks + hb
            part = rows_at(b * BLK, BLK)
            grads = edge_backward(sel[b], slope[b], dsum[part, :])
            dfar[part, :] = grads[0:BLK].astype(BF)
            down[part, :] = grads[3 * BLK :].astype(BF)
            both = grads[BLK : 3 * BLK] if both is None else both + grads[BLK : 3 * BLK]
        back[rows_at(hb * BLK, BLK), :] = both[0:BLK].astype(BF)
        back[rows_at(halo_rows + hb * BLK, BLK), :] = both[BLK:].astype(BF)
        for c, there in ((hb, below), (hblocks + hb, above)):
            part = rows_at(c * BLK, BLK)
            to_sub(back.at[part], back_in.at[part], bk_ss.at[c], bk_rs.at[c], there).start()

    def backward_dense(hb):
        parts = [rows_at((u * hblocks + hb) * BLK, BLK) for u in range(blocks // hblocks)]
        grads = jnp.concatenate([jnp.concatenate([down[p, :], dfar[p, :]], axis=1) for p in parts], axis=0)
        r = dot(jnp.concatenate([h[p, :] for p in parts], axis=0), grads, 0, 0)
        sum_f[0:128, :] += r[:, :D]
        sum_f[128:256, :] += r[:, D:]
        r = dot(grads, jnp.concatenate([wfs[...], wfo[...]], axis=1), 1, 1)
        for u, p in enumerate(parts):
            upd[p, :] += r[u * BLK : (u + 1) * BLK]

    def backward_step(hb, carry):
        backward_dense(hb - 1)
        backward_edges(hb)
        return carry

    backward_edges(0)
    lax.fori_loop(1, hblocks, backward_step, 0)
    sum_f[128:256, :] += dot(halo[...], back[...], 0, 0)
    backward_dense(hblocks - 1)
    w_f[...] = sum_f[...].astype(BF)
    weights_scatter(w_f, rs_f, f_ss, f_rs)

    grp_f[gi] = weights_sum(w_f, rs_f, f_ss, f_rs)
    fg_copies = []
    for d in range(1, n_grp):
        fg_copies.append(to_grp(grp_f.at[gi], grp_f.at[gi], fg_ss.at[d - 1], fg_rs.at[d - 1], lax.rem(gi + d, n_grp)))
        fg_copies[-1].start()
    for c in bk_copies:
        c.wait_recv()
    halo[0:halo_rows, :] = (dot(back_in[0:halo_rows, :], wfo[...], 1, 1) * has_above).astype(BF)
    halo[halo_rows:, :] = (dot(back_in[halo_rows:, :], wfo[...], 1, 1) * has_below).astype(BF)
    group = 1024

    def returned(i, carry):
        part = rows_at(i * group, group)
        hots = []
        for t in range(group // 256):
            row = []
            for table in (shi_v, slo_v):
                for l in range(halo_rows // 128):
                    row.append(group_hot(table[l : l + 1, :], i * (group // 256) + t))
            hots.append(jnp.concatenate(row, axis=1))
        grad_h[part, :] = (upd[part, :] + dot(jnp.concatenate(hots, axis=0), halo[...])).astype(BF)
        return carry

    lax.fori_loop(0, rows // group // 2, returned, 0)
    for c in fg_copies:
        c.wait_recv()
    total = grp_f[0]
    for k in range(1, n_grp):
        total = total + grp_f[k]
    weights_gather(all_f, total, fa_ss, fa_rs)
    lax.fori_loop(rows // group // 2, rows // group, returned, 0)
    stores.append(pltpu.make_async_copy(grad_h, grad_h_hbm, store_s.at[1]))
    stores[1].start()

    def finish(array, ss, rs, first, count):
        size = array.shape[0] // n_sub
        others = array.at[pl.ds(0, array.shape[0] - size)]
        to_sub(others, others, ss, rs, above).wait_recv()
        for k in range(count):
            grad_w[first + k] = array[k * 128 : (k + 1) * 128, :].astype(F32)

    finish(all_e, ea_ss, ea_rs, 3, 4)
    finish(all_f, fa_ss, fa_rs, 0, 3)

    for c in halo_copies + hist_copies + g_copies + t_copies + ch_copies + cb_copies:
        c.wait_send()
    for c in bk_copies + fg_copies:
        c.wait_send()
    for c in stores:
        c.wait()
    for received, array, ss, gather_ss, rs in ((rs_e, all_e, e_ss, ea_ss, e_rs), (rs_f, all_f, f_ss, fa_ss, f_rs)):
        to_sub(received, received, ss, rs, above).wait_send()
        others = array.at[pl.ds(0, array.shape[0] - array.shape[0] // n_sub)]
        to_sub(others, others, gather_ss, rs, above).wait_send()


def step(
    n_grp, n_sub,
    states, cotangent, fine_self, fine_other, fine_node, coarse_self, coarse_other, coarse_node, prolong,
    fine_nbr, fine_mask, fine_send_lo, fine_send_hi, coarse_nbr, coarse_mask, coarse_send_lo, coarse_send_hi, coarse_owner,
):
    rows, slots = fine_nbr.shape
    crows = coarse_nbr.shape[0]
    halo = fine_send_lo.shape[0]
    chalo = coarse_send_lo.shape[0]
    blocks, cblocks = rows // BLK, crows // BLK
    edges = BLK * slots
    vmem = pl.BlockSpec(memory_space=pltpu.VMEM)
    smem = pl.BlockSpec(memory_space=pltpu.SMEM)
    hbm = pl.BlockSpec(memory_space=pl.ANY)
    V = pltpu.VMEM
    dma = pltpu.SemaphoreType.DMA
    w_rows = 4 * D
    wc = w_rows // n_sub
    i32 = jnp.int32
    scratch = [
        V((rows, D), BF), V((rows, D), BF), V((slots, rows), i32), V((slots, rows), i32),
        V((slots, crows), i32), V((slots, crows), i32), V((rows, D), BF), V((rows, D), BF),
        V((2 * halo, D), BF), V((2 * halo, D), BF), V((2 * halo, D), BF),
        V((rows, D), BF), V((2 * halo, D), BF), V((rows, D), BF),
        V((blocks, 8, 128), F32), V((blocks, 4 * BLK, edges), BF), V((blocks, edges, D), BF),
        V((rows // TILE, crows, TILE), BF),
        V((rows, D), BF), V((rows, D), F32), V((rows, D), F32), V((crows, D), F32),
        V((16, 128), F32), V((n_grp - 1, 16, 128), F32), V((crows, D), F32),
        V((crows, D), BF), V((crows // 2, D), BF), V((crows // 2, D), BF), V((crows // 2, D), BF), V((crows, D), BF),
        V((crows, D), BF), V((crows // 2, D), BF), V((crows // 2, D), BF), V((crows // 2, D), BF), V((crows, D), BF),
        V((crows, D), F32), V((2 * chalo, D), F32), V((2 * chalo, D), BF), V((2 * chalo, D), BF), V((2 * chalo, D), BF),
        V((crows, D), BF), V((crows, D), BF), V((2 * chalo, D), BF),
        V((cblocks, 8, 128), F32), V((cblocks, 4 * BLK, edges), BF),
        V((crows, D), F32), V((crows, D), BF), V((crows, D), BF), V((crows, D), BF), V((crows, D), F32),
        V((2 * chalo, D), F32), V((2 * chalo, D), BF), V((2 * chalo, D), BF),
        V((crows, D), BF), V((crows, D), BF), V((crows, 2 * D), BF),
        V((2 * halo, D), BF), V((2 * halo, D), BF),
        V((w_rows, D), BF), V((w_rows - wc, D), BF), V((w_rows, D), BF),
        V((w_rows, D), BF), V((w_rows, D), F32), V((w_rows - wc, D), BF), V((n_grp, wc, D), F32), V((w_rows, D), BF),
        dma((6,)), dma((2,)), dma((4,)), dma((4,)),
        dma((n_grp - 1,)), dma((n_grp - 1,)), dma((3,)), dma((3,)), dma((3,)), dma((3,)),
        dma((2,)), dma((2,)), dma((2,)), dma((2,)),
        dma((2 * halo // BLK,)), dma((2 * halo // BLK,)),
        dma, dma, dma, dma,
        dma, dma, dma((n_grp - 1,)), dma((n_grp - 1,)), dma, dma,
    ]
    outs = pl.pallas_call(
        functools.partial(kernel, n_grp, n_sub),
        out_shape=(
            jax.ShapeDtypeStruct((rows, D), BF),
            jax.ShapeDtypeStruct((rows, D), BF),
            jax.ShapeDtypeStruct((7, D, D), F32),
        ),
        in_specs=[hbm] * 2 + [vmem] * 7 + [hbm] * 4 + [smem] * 4 + [vmem] * 5,
        out_specs=(hbm, hbm, vmem),
        scratch_shapes=scratch,
        compiler_params=pltpu.CompilerParams(
            collective_id=0, has_side_effects=True, vmem_limit_bytes=63 * 1024 * 1024
        ),
    )(
        states, cotangent, fine_self, fine_other, fine_node, coarse_self, coarse_other, coarse_node, prolong,
        fine_nbr.T, fine_mask.T, coarse_nbr.T, coarse_mask.T,
        fine_send_lo, fine_send_hi, coarse_send_lo, coarse_send_hi,
        fine_send_lo.reshape(-1, 128), fine_send_hi.reshape(-1, 128),
        coarse_send_lo.reshape(1, -1), coarse_send_hi.reshape(1, -1),
        coarse_owner.reshape(-1, 128),
    )
    return outs


def solution(mesh):
    rows2 = P(("grp", "sub"), None)
    rows1 = P(("grp", "sub"))
    in_specs = (
        (rows2, rows2) + (P(),) * 7
        + (rows2, rows2, rows1, rows1)
        + (P("sub", None), P("sub", None), P("sub"), P("sub"), rows1)
    )
    return jax.shard_map(
        functools.partial(step, mesh.shape["grp"], mesh.shape["sub"]),
        mesh=mesh, in_specs=in_specs, out_specs=(rows2, rows2, P()), check_vma=False,
    )
```

```python
import functools

import jax
import jax.numpy as jnp
from jax import lax
from jax.experimental import pallas as pl
from jax.experimental.pallas import tpu as pltpu
from jax.sharding import PartitionSpec as P

MESH = pl.DeviceIdType.MESH
BF = jnp.bfloat16
F32 = jnp.float32
D = 128
BLK = 64
TILE = 512


def dot(a, b, ca=1, cb=0):
    return lax.dot_general(a, b, (((ca,), (cb,)), ((), ())), preferred_element_type=F32)


def rows_at(start, size):
    if isinstance(start, int):
        return pl.ds(start, size)
    return pl.ds(pl.multiple_of(start, size if size % 8 == 0 else 8), size)


def spread(row, rows):
    one = jnp.broadcast_to(row, (16, row.shape[1])).astype(BF)
    return jnp.concatenate([one] * (rows // 16), axis=0)


def iota_bf(rows, lanes, base=0):
    return (lax.broadcasted_iota(jnp.int32, (rows, lanes), 0) + base).astype(F32).astype(BF)


def one_hot(row, rows, base=0):
    hit = iota_bf(rows, row.shape[1], base) == spread(row, rows)
    return jnp.where(hit, jnp.ones((), BF), jnp.zeros((), BF))


def group_hot(values, group):
    inside = jnp.where((values >> 8) == group, values & 255, -1).astype(F32)
    return one_hot(inside, 256)


def prepare_slots(nbr, msk, cidx, rows, halo, halo_blocks):
    def body(p, carry):
        v = nbr[:, rows_at(p * 128, 128)]
        used = msk[:, rows_at(p * 128, 128)] > 0
        lane = lax.broadcasted_iota(jnp.int32, (8, 128), 1)
        slot = lax.broadcasted_iota(jnp.int32, (8, 128), 0)
        blk = 2 * p + (lane >> 6)
        hblk = blk & (halo_blocks - 1)
        col = jnp.where(
            v < rows,
            v - blk * BLK,
            jnp.where(v < rows + halo, v - rows - hblk * BLK + BLK, v - rows - halo - hblk * BLK + 2 * BLK),
        )
        col = jnp.where(used, col, -1)
        own = jnp.where(used, 3 * BLK + (lane & (BLK - 1)), -1)
        first = lane < BLK

        def halves(x):
            later = pltpu.roll(x, 4, 0)
            return (
                jnp.where(first, x, pltpu.roll(later, BLK, 1)),
                jnp.where(first, pltpu.roll(x, BLK, 1), later),
            )

        for half, (c, o) in enumerate(zip(halves(col), halves(own))):
            cidx[2 * p + half] = jnp.where(slot < 4, c, pltpu.roll(o, 4, 0)).astype(F32)
        return carry

    lax.fori_loop(0, rows // 128, body, 0)


def build_selectors(cidx, sel, blocks):
    def body(p, carry):
        for u in range(4):
            b = p * 4 + u
            idx = cidx[b]
            for j in range(4):
                sel[b, 0 : 3 * BLK, j * 128 : (j + 1) * 128] = one_hot(idx[j : j + 1], 3 * BLK)
                sel[b, 3 * BLK : 4 * BLK, j * 128 : (j + 1) * 128] = one_hot(idx[4 + j : 5 + j], BLK, 3 * BLK)
        return carry

    lax.fori_loop(0, blocks // 4, body, 0)


def gather_rows(index, source, staged, start, count):
    def body(i, carry):
        at = pl.multiple_of(start + i * 16, 16)
        for u in range(16):
            staged[pl.ds(at + u, 1), :] = source[pl.ds(index[i * 16 + u], 1), :]
        return carry

    lax.fori_loop(0, count // 16, body, 0)


def edge_forward(sel, window):
    half = dot(sel, window, 0, 0)
    up = 1.0 + jnp.tanh(half)
    act = half * up
    slope = (up + act * (2.0 - up)).astype(BF)
    total = act[0:BLK]
    for k in range(1, 8):
        total = total + act[k * BLK : (k + 1) * BLK]
    return total, slope


def edge_backward(sel, slope, half_grad):
    grad = jnp.concatenate([half_grad] * 8, axis=0) * slope
    return dot(sel, grad)


def kernel(
    n_grp, n_sub,
    h_hbm, g_hbm, wfs, wfo, wfn, wcs, wco, wcn, wpr, nbr_hbm, msk_hbm, cnbr_hbm, cmsk_hbm,
    slo_s, shi_s, cslo_s, cshi_s, slo_v, shi_v, cslo_v, cshi_v, owner,
    result_hbm, grad_h_hbm, grad_w,
    h, g, nbr, msk, cnbr, cmsk, result, grad_h,
    stage, halo_in, halo, far_dfar, farh, own_dsum, cidx, sel, slope, st, summed, down, upd, rowbuf, acc,
    hist, hist_in, rcnt, gsend, gcore, gchip, gx, gall, tsend, tcore, tchip, tx, cin, cinf, cstaged, cstage, chalo_in, chalo, cown, cfar, cfarh,
    ccidx, csel, yc, dsc, csum, cdown, cdfar, chacc, cback, cback_in, cout, cprol, mm, back, back_in,
    w_e, rs_e, line_e, all_e, w_f, sum_f, rs_f, line_f, all_f,
    load_s, store_s, halo_ss, halo_rs, hist_ss, hist_rs, gs_ss, gs_rs, ts_ss, ts_rs,
    ch_ss, ch_rs, cb_ss, cb_rs, bk_ss, bk_rs, e_ss, e_rs, el_ss, el_rs, ea_ss, ea_rs, f_ss, f_rs, fl_ss, fl_rs, fa_ss, fa_rs,
):
    own, dsum = own_dsum, own_dsum
    far, dfar = far_dfar, far_dfar
    gw = rowbuf
    rows = h.shape[0]
    crows = cnbr.shape[1]
    halo_rows = shi_s.shape[0]
    chalo_rows = cshi_s.shape[0]
    tiles = rows // TILE
    blocks = rows // BLK
    cblocks = crows // BLK
    hblocks = halo_rows // BLK
    gi = lax.axis_index("grp")
    si = lax.axis_index("sub")
    above = lax.rem(si + 1, n_sub)
    below = lax.rem(si + n_sub - 1, n_sub)
    core = lax.rem(gi, 2)
    sibling = gi + 1 - 2 * core
    other_chip = lax.rem(gi + 2, n_grp)
    has_below = jnp.where(si > 0, 1.0, 0.0).astype(F32)
    has_above = jnp.where(si < n_sub - 1, 1.0, 0.0).astype(F32)

    def to_sub(src, dst, ss, rs, there):
        return pltpu.make_async_remote_copy(
            src_ref=src, dst_ref=dst, send_sem=ss, recv_sem=rs, device_id={"sub": there}, device_id_type=MESH
        )

    def to_grp(src, dst, ss, rs, there):
        return pltpu.make_async_remote_copy(
            src_ref=src, dst_ref=dst, send_sem=ss, recv_sem=rs, device_id={"grp": there}, device_id_type=MESH
        )

    loads = []
    for k, (src, dst) in enumerate(
        ((h_hbm, h), (g_hbm, g), (nbr_hbm, nbr), (msk_hbm, msk), (cnbr_hbm, cnbr), (cmsk_hbm, cmsk))
    ):
        loads.append(pltpu.make_async_copy(src, dst, load_s.at[k]))
        loads[-1].start()

    plane = n_sub // 2
    line = lax.rem(si, 2)
    yz = si // 2

    def in_plane(d):
        there = lax.rem(yz + d, plane)
        return there, there * 2 + line

    def weights_scatter(array, received, ss, rs):
        size = array.shape[0] // plane

        def body(d, carry):
            chunk, there = in_plane(d)
            to_sub(array.at[rows_at(chunk * size, size)], received.at[rows_at((d - 1) * size, size)], ss, rs, there).start()
            return carry

        lax.fori_loop(1, plane, body, 0)

    def weights_line(array, received, lines, ss, rs, line_ss, line_rs):
        size = array.shape[0] // plane
        to_sub(received, received, ss, rs, above).wait_recv()

        def body(d, total):
            return total + received[rows_at((d - 1) * size, size), :].astype(F32)

        total = lax.fori_loop(1, plane, body, array[rows_at(yz * size, size), :].astype(F32))
        groups = lines.shape[0] // 2
        mine = line * groups + (gi if groups > 1 else 0)
        lines[mine] = total.astype(BF)
        copies = []
        for k in range(1, 2 * groups):
            sub_there = si if k < groups else si + 1 - 2 * line
            grp_there = lax.rem(gi + k, n_grp) if groups > 1 else gi
            copies.append(
                pltpu.make_async_remote_copy(
                    src_ref=lines.at[mine], dst_ref=lines.at[mine], send_sem=line_ss.at[k - 1], recv_sem=line_rs.at[k - 1],
                    device_id={"grp": grp_there, "sub": sub_there}, device_id_type=MESH,
                )
            )
            copies[-1].start()
        return copies

    def weights_gather(array, lines, copies, ss, rs):
        size = array.shape[0] // plane
        for c in copies:
            c.wait_recv()
        total = lines[0].astype(F32)
        for k in range(1, lines.shape[0]):
            total = total + lines[k].astype(F32)
        mine = rows_at(yz * size, size)
        array[mine, :] = total.astype(BF)

        def body(d, carry):
            to_sub(array.at[mine], array.at[mine], ss, rs, in_plane(d)[1]).start()
            return carry

        lax.fori_loop(1, plane, body, 0)

    barrier = pltpu.get_barrier_semaphore()

    def greet(sub_there, grp_there):
        pl.semaphore_signal(barrier, inc=1, device_id={"grp": grp_there, "sub": sub_there}, device_id_type=MESH)

    def greet_plane(d, carry):
        greet(in_plane(d)[1], gi)
        return carry

    lax.fori_loop(1, plane, greet_plane, 0)
    for k in range(1, 2 * n_grp):
        greet(si if k < n_grp else si + 1 - 2 * line, lax.rem(gi + k, n_grp))
    for there in (above, below):
        greet(there, gi)
        greet(there, sibling)

    def widen(i, carry):
        upd[rows_at(i * TILE, TILE), :] = h[rows_at(i * TILE, TILE), :].astype(F32)
        return carry

    loads[0].wait()
    lax.fori_loop(0, tiles, widen, 0)
    gather_rows(shi_s, upd, rowbuf, 0, halo_rows)
    gather_rows(slo_s, upd, rowbuf, halo_rows, halo_rows)
    stage[...] = rowbuf[0 : 2 * halo_rows, :].astype(BF)
    pl.semaphore_wait(barrier, plane - 1 + 2 * n_grp - 1 + 4)
    half = halo_rows // 2
    halo_copies = []
    for c in range(4):
        part = pl.ds(c * half, half)
        halo_copies.append(
            to_sub(stage.at[part], halo_in.at[part], halo_ss.at[c], halo_rs.at[c], above if c < 2 else below)
        )
        halo_copies[-1].start()

    loads[1].wait()
    acc[...] = jnp.zeros_like(acc)
    hist[...] = jnp.zeros_like(hist)

    def owners(i, carry):
        high, low = [], []
        for l in range(TILE // 128):
            v = owner[pl.ds(i * (TILE // 128) + l, 1), :]
            for t in range(crows // 256):
                st[i, t * 256 : (t + 1) * 256, l * 128 : (l + 1) * 128] = group_hot(v, t)
            high.append(one_hot((v >> 7).astype(F32), 16))
            low.append(one_hot((v & 127).astype(F32), 128))
        hist[...] += dot(jnp.concatenate(high, axis=1), jnp.concatenate(low, axis=1), 1, 1)
        acc[...] += dot(st[i], g[rows_at(i * TILE, TILE), :])
        return carry

    lax.fori_loop(0, tiles, owners, 0)
    hist_copies = []
    for d in range(1, n_grp):
        hist_copies.append(
            to_grp(hist, hist_in.at[d - 1], hist_ss.at[d - 1], hist_rs.at[d - 1], lax.rem(gi + d, n_grp))
        )
        hist_copies[-1].start()

    part_rows = crows // 2
    mine = rows_at(core * part_rows, part_rows)
    theirs = rows_at((1 - core) * part_rows, part_rows)

    def group_first(sums, send, received, ss, rs):
        send[...] = sums[theirs, :].astype(BF)
        copy = to_grp(send, received, ss.at[0], rs.at[0], sibling)
        copy.start()
        return [copy]

    def group_second(copies, sums, received, chip, other, ss, rs):
        copies[0].wait_recv()
        chip[...] = (sums[mine, :] + received[...].astype(F32)).astype(BF)
        copies.append(to_grp(chip, other, ss.at[1], rs.at[1], other_chip))
        copies[1].start()

    def group_third(copies, chip, other, scale, whole, ss, rs):
        copies[1].wait_recv()
        total = chip[...].astype(F32) + other[...].astype(F32)
        whole[mine, :] = (total if scale is None else total * scale[mine, :]).astype(BF)
        copies.append(to_grp(whole.at[mine], whole.at[mine], ss.at[2], rs.at[2], sibling))
        copies[2].start()

    g_copies = group_first(acc, gsend, gcore, gs_ss, gs_rs)

    for c in loads[2:]:
        c.wait()
    prepare_slots(nbr, msk, cidx, rows, halo_rows, hblocks)
    both_f = jnp.concatenate([wfs[...] * 0.5, wfo[...] * 0.5], axis=1)

    def dense(i, carry):
        part = rows_at(i * TILE, TILE)
        r = dot(h[part, :], both_f)
        own[part, :] = r[:, :D].astype(BF)
        far[part, :] = r[:, D:].astype(BF)
        return carry

    lax.fori_loop(0, tiles, dense, 0)
    build_selectors(cidx, sel, blocks)

    group_second(g_copies, acc, gcore, gchip, gx, gs_ss, gs_rs)

    for c in halo_copies:
        c.wait_recv()
    halo[0:halo_rows, :] = (halo_in[0:halo_rows, :].astype(F32) * has_below).astype(BF)
    halo[halo_rows:, :] = (halo_in[halo_rows:, :].astype(F32) * has_above).astype(BF)
    farh[...] = dot(halo[...], wfo[...] * 0.5).astype(BF)

    acc[...] = jnp.zeros_like(acc)

    def forward_edges(i):
        for u in range(TILE // BLK):
            b = i * (TILE // BLK) + u
            hb = b & (hblocks - 1)
            window = jnp.concatenate(
                [
                    far[rows_at(b * BLK, BLK), :],
                    farh[rows_at(hb * BLK, BLK), :],
                    farh[rows_at(halo_rows + hb * BLK, BLK), :],
                    own[rows_at(b * BLK, BLK), :],
                ],
                axis=0,
            )
            total, q = edge_forward(sel[b], window)
            slope[b] = q
            summed[rows_at(b * BLK, BLK), :] = total.astype(BF)

    def forward_new(i):
        part = rows_at(i * TILE, TILE)
        new = h[part, :].astype(F32) + dot(summed[part, :], wfn[...])
        upd[part, :] = new
        return new.astype(BF)

    def forward_update(i):
        acc[...] += dot(st[i], forward_new(i))

    def forward_tiles(p, carry):
        forward_update(p * 2 - 2)
        forward_update(p * 2 - 1)
        forward_edges(p * 2)
        forward_edges(p * 2 + 1)
        return carry

    forward_edges(0)
    forward_edges(1)
    lax.fori_loop(1, tiles // 2, forward_tiles, 0)
    new_a, new_b = forward_new(tiles - 2), forward_new(tiles - 1)
    acc[theirs, :] += dot(st[tiles - 2, theirs, :], new_a) + dot(st[tiles - 1, theirs, :], new_b)

    t_copies = group_first(acc, tsend, tcore, ts_ss, ts_rs)
    acc[mine, :] += dot(st[tiles - 2, mine, :], new_a) + dot(st[tiles - 1, mine, :], new_b)
    group_third(g_copies, gchip, gx, None, gall, gs_ss, gs_rs)
    for c in hist_copies:
        c.wait_recv()
    counts = hist[...]
    for d in range(1, n_grp):
        counts = counts + hist_in[d - 1]
    for k in range(crows // 128):
        rcnt[k * 128 : (k + 1) * 128, :] = 1.0 / jnp.maximum(
            jnp.transpose(jnp.broadcast_to(counts[k : k + 1], (128, 128))), 1.0
        )
    prepare_slots(cnbr, cmsk, ccidx, crows, chalo_rows, 1)
    g_copies[2].wait_recv()
    yc[...] = dot(gall[...], wpr[...], 1, 1)
    group_second(t_copies, acc, tcore, tchip, tx, ts_ss, ts_rs)
    dsc[...] = (dot(yc[...].astype(BF), wcn[...], 1, 1) * 0.5).astype(BF)
    build_selectors(ccidx, csel, cblocks)
    group_third(t_copies, tchip, tx, rcnt, cin, ts_ss, ts_rs)
    cinf[mine, :] = cin[mine, :].astype(F32)
    cinf[theirs, :] = jnp.zeros((part_rows, D), F32)
    gather_rows(cshi_s, cinf, cstaged, 0, chalo_rows)
    gather_rows(cslo_s, cinf, cstaged, chalo_rows, chalo_rows)
    cstage[...] = cstaged[...].astype(BF)
    ch_copies = []
    for c in range(4):
        part = pl.ds((c // 2) * chalo_rows, chalo_rows)
        ch_copies.append(
            pltpu.make_async_remote_copy(
                src_ref=cstage.at[part], dst_ref=chalo_in.at[c % 2, part], send_sem=ch_ss.at[c], recv_sem=ch_rs.at[c],
                device_id={"grp": (gi, sibling)[c % 2], "sub": (above, below)[c // 2]}, device_id_type=MESH,
            )
        )
        ch_copies[-1].start()
    t_copies[2].wait_recv()
    r = dot(cin[...], jnp.concatenate([wcs[...] * 0.5, wco[...] * 0.5], axis=1))
    cown[...] = r[:, :D].astype(BF)
    cfar[...] = r[:, D:].astype(BF)

    def known_part(i, carry):
        part = rows_at(i * TILE, TILE)
        gw[part, :] = dot(g[part, :], wfn[...], 1, 1) * 0.5
        return carry

    lax.fori_loop(0, tiles, known_part, 0)
    for c in ch_copies:
        c.wait_recv()
    arrived = chalo_in[0].astype(F32) + chalo_in[1].astype(F32)
    chalo[0:chalo_rows, :] = (arrived[0:chalo_rows] * has_below).astype(BF)
    chalo[chalo_rows:, :] = (arrived[chalo_rows:] * has_above).astype(BF)
    cfarh[...] = dot(chalo[...], wco[...] * 0.5).astype(BF)
    chacc[...] = jnp.zeros_like(chacc)

    def mid_blocks(p, carry):
        both = None
        for u in range(8):
            b = p * 8 + u
            part = rows_at(b * BLK, BLK)
            total, q = edge_forward(csel[b], jnp.concatenate([cfar[part, :], cfarh[...], cown[part, :]], axis=0))
            csum[part, :] = total.astype(BF)
            grads = edge_backward(csel[b], q, dsc[part, :])
            cdfar[part, :] = grads[0:BLK]
            both = grads[BLK : 3 * BLK] if both is None else both + grads[BLK : 3 * BLK]
            cdown[part, :] = grads[3 * BLK :].astype(BF)
        chacc[...] += both
        return carry

    lax.fori_loop(0, cblocks // 8, mid_blocks, 0)
    cback[...] = chacc[...].astype(BF)
    cb_copies = []
    for c in range(2):
        part = pl.ds(c * chalo_rows, chalo_rows)
        cb_copies.append(to_sub(cback.at[part], cback_in.at[part], cb_ss.at[c], cb_rs.at[c], (below, above)[c]))
        cb_copies[-1].start()

    cout[...] = (cin[...].astype(F32) + dot(csum[...], wcn[...])).astype(BF)
    cprol[...] = dot(cout[...], wpr[...]).astype(BF)

    r = dot(cin[...], jnp.concatenate([cdown[...], cdfar[...].astype(BF)], axis=1), 0, 0)
    w_e[0:128, :] = r[:, :D].astype(BF)
    w_e[128:256, :] = (r[:, D:] + dot(chalo[...], cback[...], 0, 0)).astype(BF)
    w_e[256:384, :] = dot(csum[...], yc[...].astype(BF), 0, 0).astype(BF)
    w_e[384:512, :] = dot(cout[...], gall[...], 0, 0).astype(BF)
    weights_scatter(w_e, rs_e, e_ss, e_rs)

    def prolonged(p, carry):
        for u in range(2):
            i = p * 2 + u
            part = rows_at(i * TILE, TILE)
            result[part, :] = (upd[part, :] + dot(st[i], cprol[...], 0, 0)).astype(BF)
        return carry

    lax.fori_loop(0, tiles // 2, prolonged, 0)
    stores = [pltpu.make_async_copy(result, result_hbm, store_s.at[0])]
    stores[0].start()
    for c in cb_copies:
        c.wait_recv()
    from_above = (cback_in[0:chalo_rows, :].astype(F32) * has_above).astype(BF)
    from_below = (cback_in[chalo_rows:, :].astype(F32) * has_below).astype(BF)
    for t in range(crows // 256):
        part = slice(t * 256, (t + 1) * 256)
        cdfar[part, :] += dot(group_hot(cshi_v[...], t), from_above) + dot(group_hot(cslo_v[...], t), from_below)
    dcin = yc[...] + dot(cdown[...], wcs[...], 1, 1) + dot(cdfar[...].astype(BF), wco[...], 1, 1)
    m = (dcin * rcnt[...]).astype(BF)
    mm[:, :D] = m
    mm[:, D:] = (dot(m, wfn[...], 1, 1) * 0.5).astype(BF)

    sum_f[...] = jnp.zeros_like(sum_f)

    def cotangents(p, carry):
        for u in range(2):
            i = p * 2 + u
            part = rows_at(i * TILE, TILE)
            r = dot(st[i], mm[...], 0, 0)
            y = g[part, :].astype(F32) + r[:, :D]
            upd[part, :] = y
            dsum[part, :] = (gw[part, :] + r[:, D:]).astype(BF)
        return carry

    lax.fori_loop(0, tiles // 2, cotangents, 0)

    e_copies = weights_line(w_e, rs_e, line_e, e_ss, e_rs, el_ss, el_rs)

    bk_copies = []
    for c in range(2 * hblocks):
        part = pl.ds(c * BLK, BLK)
        bk_copies.append(
            to_sub(back.at[part], back_in.at[part], bk_ss.at[c], bk_rs.at[c], below if c < hblocks else above)
        )

    def backward_edges(hb):
        both = None
        for u in range(blocks // hblocks):
            b = u * hblocks + hb
            part = rows_at(b * BLK, BLK)
            grads = edge_backward(sel[b], slope[b], dsum[part, :])
            dfar[part, :] = grads[0:BLK].astype(BF)
            down[part, :] = grads[3 * BLK :].astype(BF)
            both = grads[BLK : 3 * BLK] if both is None else both + grads[BLK : 3 * BLK]
        back[rows_at(hb * BLK, BLK), :] = both[0:BLK].astype(BF)
        back[rows_at(halo_rows + hb * BLK, BLK), :] = both[BLK:].astype(BF)
        for c, there in ((hb, below), (hblocks + hb, above)):
            part = rows_at(c * BLK, BLK)
            to_sub(back.at[part], back_in.at[part], bk_ss.at[c], bk_rs.at[c], there).start()

    def backward_weights(hb):
        parts = [rows_at((u * hblocks + hb) * BLK, BLK) for u in range(blocks // hblocks)]
        grads = jnp.concatenate([jnp.concatenate([down[p, :], dfar[p, :]], axis=1) for p in parts], axis=0)
        r = dot(jnp.concatenate([h[p, :] for p in parts], axis=0), grads, 0, 0)
        below_part = rows_at(hb * BLK, BLK)
        above_part = rows_at(halo_rows + hb * BLK, BLK)
        halo_grad = jnp.concatenate([back[below_part, :], back[above_part, :]], axis=0)
        halo_row = jnp.concatenate([halo[below_part, :], halo[above_part, :]], axis=0)
        sum_f[0:128, :] += r[:, :D]
        sum_f[128:256, :] += r[:, D:] + dot(halo_row, halo_grad, 0, 0)
        y = jnp.concatenate([upd[p, :] for p in parts], axis=0)
        sum_f[256:384, :] += dot(jnp.concatenate([summed[p, :] for p in parts], axis=0), y.astype(BF), 0, 0)
        return parts, grads, y

    def backward_latents(parts, grads, y):
        r = dot(grads, jnp.concatenate([wfs[...], wfo[...]], axis=1), 1, 1) + y
        for u, p in enumerate(parts):
            upd[p, :] = r[u * BLK : (u + 1) * BLK]

    def backward_step(hb, carry):
        backward_latents(*backward_weights(hb - 1))
        backward_edges(hb)
        return carry

    backward_edges(0)
    lax.fori_loop(1, hblocks, backward_step, 0)
    last = backward_weights(hblocks - 1)
    w_f[...] = sum_f[...].astype(BF)
    weights_scatter(w_f, rs_f, f_ss, f_rs)
    weights_gather(all_e, line_e, e_copies, ea_ss, ea_rs)
    backward_latents(*last)


    f_copies = weights_line(w_f, rs_f, line_f, f_ss, f_rs, fl_ss, fl_rs)

    for c in bk_copies:
        c.wait_recv()
    halo[0:halo_rows, :] = (dot(back_in[0:halo_rows, :], wfo[...], 1, 1) * has_above).astype(BF)
    halo[halo_rows:, :] = (dot(back_in[halo_rows:, :], wfo[...], 1, 1) * has_below).astype(BF)
    group = 1024

    def returned(i, carry):
        part = rows_at(i * group, group)
        hots = []
        for t in range(group // 256):
            row = []
            for table in (shi_v, slo_v):
                for l in range(halo_rows // 128):
                    row.append(group_hot(table[l : l + 1, :], i * (group // 256) + t))
            hots.append(jnp.concatenate(row, axis=1))
        grad_h[part, :] = (upd[part, :] + dot(jnp.concatenate(hots, axis=0), halo[...])).astype(BF)
        return carry

    def store_half(k):
        part = pl.ds(k * (rows // 2), rows // 2)
        stores.append(pltpu.make_async_copy(grad_h.at[part], grad_h_hbm.at[part], store_s.at[1 + k]))
        stores[-1].start()

    lax.fori_loop(0, rows // group // 2, returned, 0)
    store_half(0)
    weights_gather(all_f, line_f, f_copies, fa_ss, fa_rs)
    lax.fori_loop(rows // group // 2, rows // group, returned, 0)
    store_half(1)

    def finish(array, ss, rs, first, count):
        size = array.shape[0] // plane
        others = array.at[pl.ds(0, array.shape[0] - size)]
        to_sub(others, others, ss, rs, above).wait_recv()
        for k in range(count):
            grad_w[first + k] = array[k * 128 : (k + 1) * 128, :].astype(F32)

    finish(all_f, fa_ss, fa_rs, 0, 3)
    finish(all_e, ea_ss, ea_rs, 3, 4)

    for c in halo_copies + hist_copies + g_copies + t_copies + ch_copies + cb_copies:
        c.wait_send()
    for c in bk_copies + f_copies + e_copies:
        c.wait_send()
    for c in stores:
        c.wait()
    for received, array, ss, gather_ss, rs in ((rs_e, all_e, e_ss, ea_ss, e_rs), (rs_f, all_f, f_ss, fa_ss, f_rs)):
        to_sub(received, received, ss, rs, above).wait_send()
        others = array.at[pl.ds(0, array.shape[0] - array.shape[0] // plane)]
        to_sub(others, others, gather_ss, rs, above).wait_send()


def step(
    n_grp, n_sub,
    states, cotangent, fine_self, fine_other, fine_node, coarse_self, coarse_other, coarse_node, prolong,
    fine_nbr, fine_mask, fine_send_lo, fine_send_hi, coarse_nbr, coarse_mask, coarse_send_lo, coarse_send_hi, coarse_owner,
):
    rows, slots = fine_nbr.shape
    crows = coarse_nbr.shape[0]
    halo = fine_send_lo.shape[0]
    chalo = coarse_send_lo.shape[0]
    blocks, cblocks = rows // BLK, crows // BLK
    edges = BLK * slots
    vmem = pl.BlockSpec(memory_space=pltpu.VMEM)
    smem = pl.BlockSpec(memory_space=pltpu.SMEM)
    hbm = pl.BlockSpec(memory_space=pl.ANY)
    V = pltpu.VMEM
    dma = pltpu.SemaphoreType.DMA
    w_rows = 4 * D
    wc = w_rows // (n_sub // 2)
    i32 = jnp.int32
    scratch = [
        V((rows, D), BF), V((rows, D), BF), V((slots, rows), i32), V((slots, rows), i32),
        V((slots, crows), i32), V((slots, crows), i32), V((rows, D), BF), V((rows, D), BF),
        V((2 * halo, D), BF), V((2 * halo, D), BF), V((2 * halo, D), BF),
        V((rows, D), BF), V((2 * halo, D), BF), V((rows, D), BF),
        V((blocks, 8, 128), F32), V((blocks, 4 * BLK, edges), BF), V((blocks, edges, D), BF),
        V((rows // TILE, crows, TILE), BF),
        V((rows, D), BF), V((rows, D), BF), V((rows, D), F32), V((rows, D), F32), V((crows, D), F32),
        V((16, 128), F32), V((n_grp - 1, 16, 128), F32), V((crows, D), F32),
        V((crows // 2, D), BF), V((crows // 2, D), BF), V((crows // 2, D), BF), V((crows // 2, D), BF), V((crows, D), BF),
        V((crows // 2, D), BF), V((crows // 2, D), BF), V((crows // 2, D), BF), V((crows // 2, D), BF), V((crows, D), BF),
        V((crows, D), F32), V((2 * chalo, D), F32), V((2 * chalo, D), BF), V((2, 2 * chalo, D), BF), V((2 * chalo, D), BF),
        V((crows, D), BF), V((crows, D), BF), V((2 * chalo, D), BF),
        V((cblocks, 8, 128), F32), V((cblocks, 4 * BLK, edges), BF),
        V((crows, D), F32), V((crows, D), BF), V((crows, D), BF), V((crows, D), BF), V((crows, D), F32),
        V((2 * chalo, D), F32), V((2 * chalo, D), BF), V((2 * chalo, D), BF),
        V((crows, D), BF), V((crows, D), BF), V((crows, 2 * D), BF),
        V((2 * halo, D), BF), V((2 * halo, D), BF),
        V((w_rows, D), BF), V((w_rows - wc, D), BF), V((2, wc, D), BF), V((w_rows, D), BF),
        V((w_rows, D), BF), V((w_rows, D), F32), V((w_rows - wc, D), BF), V((2 * n_grp, wc, D), BF), V((w_rows, D), BF),
        dma((6,)), dma((3,)), dma((4,)), dma((4,)),
        dma((n_grp - 1,)), dma((n_grp - 1,)), dma((3,)), dma((3,)), dma((3,)), dma((3,)),
        dma((4,)), dma((4,)), dma((2,)), dma((2,)),
        dma((2 * halo // BLK,)), dma((2 * halo // BLK,)),
        dma, dma, dma((1,)), dma((1,)), dma, dma,
        dma, dma, dma((2 * n_grp - 1,)), dma((2 * n_grp - 1,)), dma, dma,
    ]
    outs = pl.pallas_call(
        functools.partial(kernel, n_grp, n_sub),
        out_shape=(
            jax.ShapeDtypeStruct((rows, D), BF),
            jax.ShapeDtypeStruct((rows, D), BF),
            jax.ShapeDtypeStruct((7, D, D), F32),
        ),
        in_specs=[hbm] * 2 + [vmem] * 7 + [hbm] * 4 + [smem] * 4 + [vmem] * 5,
        out_specs=(hbm, hbm, vmem),
        scratch_shapes=scratch,
        compiler_params=pltpu.CompilerParams(
            collective_id=0, has_side_effects=True, vmem_limit_bytes=63 * 1024 * 1024
        ),
    )(
        states, cotangent, fine_self, fine_other, fine_node, coarse_self, coarse_other, coarse_node, prolong,
        fine_nbr.T, fine_mask.T, coarse_nbr.T, coarse_mask.T,
        fine_send_lo, fine_send_hi, coarse_send_lo, coarse_send_hi,
        fine_send_lo.reshape(-1, 128), fine_send_hi.reshape(-1, 128),
        coarse_send_lo.reshape(1, -1), coarse_send_hi.reshape(1, -1),
        coarse_owner.reshape(-1, 128),
    )
    return outs


def solution(mesh):
    rows2 = P(("grp", "sub"), None)
    rows1 = P(("grp", "sub"))
    in_specs = (
        (rows2, rows2) + (P(),) * 7
        + (rows2, rows2, rows1, rows1)
        + (P("sub", None), P("sub", None), P("sub"), P("sub"), rows1)
    )
    return jax.shard_map(
        functools.partial(step, mesh.shape["grp"], mesh.shape["sub"]),
        mesh=mesh, in_specs=in_specs, out_specs=(rows2, rows2, P()), check_vma=False,
    )
```

```python
import functools

import jax
import jax.numpy as jnp
from jax import lax
from jax.experimental import pallas as pl
from jax.experimental.pallas import tpu as pltpu
from jax.sharding import PartitionSpec as P

MESH = pl.DeviceIdType.MESH
BF = jnp.bfloat16
F32 = jnp.float32
D = 128
BLK = 64
TILE = 512


def dot(a, b, ca=1, cb=0):
    return lax.dot_general(a, b, (((ca,), (cb,)), ((), ())), preferred_element_type=F32)


def rows_at(start, size):
    if isinstance(start, int):
        return pl.ds(start, size)
    return pl.ds(pl.multiple_of(start, size if size % 8 == 0 else 8), size)


def spread(row, rows):
    one = jnp.broadcast_to(row, (16, row.shape[1])).astype(BF)
    return jnp.concatenate([one] * (rows // 16), axis=0)


def iota_bf(rows, lanes, base=0):
    return (lax.broadcasted_iota(jnp.int32, (rows, lanes), 0) + base).astype(F32).astype(BF)


def one_hot(row, rows, base=0):
    hit = iota_bf(rows, row.shape[1], base) == spread(row, rows)
    return jnp.where(hit, jnp.ones((), BF), jnp.zeros((), BF))


def group_hot(values, group):
    inside = jnp.where((values >> 8) == group, values & 255, -1).astype(F32)
    return one_hot(inside, 256)


def prepare_slots(nbr, msk, cidx, rows, halo, halo_blocks):
    def body(p, carry):
        v = nbr[:, rows_at(p * 128, 128)]
        used = msk[:, rows_at(p * 128, 128)] > 0
        lane = lax.broadcasted_iota(jnp.int32, (8, 128), 1)
        slot = lax.broadcasted_iota(jnp.int32, (8, 128), 0)
        blk = 2 * p + (lane >> 6)
        hblk = blk & (halo_blocks - 1)
        col = jnp.where(
            v < rows,
            v - blk * BLK,
            jnp.where(v < rows + halo, v - rows - hblk * BLK + BLK, v - rows - halo - hblk * BLK + 2 * BLK),
        )
        col = jnp.where(used, col, -1)
        own = jnp.where(used, 3 * BLK + (lane & (BLK - 1)), -1)
        first = lane < BLK

        def halves(x):
            later = pltpu.roll(x, 4, 0)
            return (
                jnp.where(first, x, pltpu.roll(later, BLK, 1)),
                jnp.where(first, pltpu.roll(x, BLK, 1), later),
            )

        for half, (c, o) in enumerate(zip(halves(col), halves(own))):
            cidx[2 * p + half] = jnp.where(slot < 4, c, pltpu.roll(o, 4, 0)).astype(F32)
        return carry

    lax.fori_loop(0, rows // 128, body, 0)


def build_selectors(cidx, sel, blocks):
    def body(p, carry):
        for u in range(4):
            b = p * 4 + u
            idx = cidx[b]
            for j in range(4):
                sel[b, 0 : 3 * BLK, j * 128 : (j + 1) * 128] = one_hot(idx[j : j + 1], 3 * BLK)
                sel[b, 3 * BLK : 4 * BLK, j * 128 : (j + 1) * 128] = one_hot(idx[4 + j : 5 + j], BLK, 3 * BLK)
        return carry

    lax.fori_loop(0, blocks // 4, body, 0)


def gather_rows(index, source, staged, start, count):
    def body(i, carry):
        at = pl.multiple_of(start + i * 16, 16)
        for u in range(16):
            staged[pl.ds(at + u, 1), :] = source[pl.ds(index[i * 16 + u], 1), :]
        return carry

    lax.fori_loop(0, count // 16, body, 0)


def edge_forward(sel, window):
    half = dot(sel, window, 0, 0)
    up = 1.0 + jnp.tanh(half)
    act = half * up
    slope = (up + act * (2.0 - up)).astype(BF)
    total = act[0:BLK]
    for k in range(1, 8):
        total = total + act[k * BLK : (k + 1) * BLK]
    return total, slope


def edge_backward(sel, slope, half_grad):
    grad = jnp.concatenate([half_grad] * 8, axis=0) * slope
    return dot(sel, grad)


def copy_kernel(*refs):
    count = len(refs) // 2
    for k in range(count):
        refs[count + k][...] = refs[k][...].astype(refs[count + k].dtype)


def copied(arrays, steps):
    specs = []
    for a in arrays:
        if a.ndim == 2:
            specs.append(pl.BlockSpec((a.shape[0] // steps, a.shape[1]), lambda i: (i, 0)))
        else:
            specs.append(pl.BlockSpec((a.shape[0], a.shape[1] // steps, a.shape[2]), lambda i: (0, i, 0)))
    return pl.pallas_call(
        copy_kernel,
        grid=(steps,),
        out_shape=tuple(jax.ShapeDtypeStruct(a.shape, BF if a.ndim == 2 else F32) for a in arrays),
        in_specs=specs,
        out_specs=tuple(specs),
    )(*arrays)


def kernel(
    n_grp, n_sub,
    h_hbm, g_hbm, wfs, wfo, wfn, wcs, wco, wcn, wpr, nbr_hbm, msk_hbm, cnbr_hbm, cmsk_hbm,
    slo_s, shi_s, cslo_s, cshi_s, slo_v, shi_v, cslo_v, cshi_v, owner,
    result_hbm, grad_h_hbm, grad_w_hbm,
    h, g, nbr, msk, cnbr, cmsk, result, grad_h,
    stage, halo_in, halo, far_dfar, farh, own_dsum, cidx, sel, slope, st, summed, down, upd, rowbuf, acc,
    hist, hist_in, rcnt, gsend, gcore, gchip, gx, gall, tsend, tcore, tchip, tx, cin, cinf, cstaged, cstage, chalo_in, chalo, cown, cfar, cfarh,
    ccidx, csel, yc, dsc, csum, cdown, cdfar, chacc, cback, cback_in, cout, cprol, mm, back, back_in,
    w_e, rs_e, line_e, all_e, w_f, sum_f, rs_f, line_f, all_f,
    load_s, store_s, halo_ss, halo_rs, hist_ss, hist_rs, gs_ss, gs_rs, ts_ss, ts_rs,
    ch_ss, ch_rs, cb_ss, cb_rs, bk_ss, bk_rs, e_ss, e_rs, el_ss, el_rs, ea_ss, ea_rs, f_ss, f_rs, fl_ss, fl_rs, fa_ss, fa_rs,
):
    own, dsum = own_dsum, own_dsum
    far, dfar = far_dfar, far_dfar
    gw = rowbuf
    rows = h.shape[0]
    crows = cnbr.shape[1]
    halo_rows = shi_s.shape[0]
    chalo_rows = cshi_s.shape[0]
    tiles = rows // TILE
    blocks = rows // BLK
    cblocks = crows // BLK
    hblocks = halo_rows // BLK
    gi = lax.axis_index("grp")
    si = lax.axis_index("sub")
    above = lax.rem(si + 1, n_sub)
    below = lax.rem(si + n_sub - 1, n_sub)
    core = lax.rem(gi, 2)
    sibling = gi + 1 - 2 * core
    other_chip = lax.rem(gi + 2, n_grp)
    has_below = jnp.where(si > 0, 1.0, 0.0).astype(F32)
    has_above = jnp.where(si < n_sub - 1, 1.0, 0.0).astype(F32)

    def to_sub(src, dst, ss, rs, there):
        return pltpu.make_async_remote_copy(
            src_ref=src, dst_ref=dst, send_sem=ss, recv_sem=rs, device_id={"sub": there}, device_id_type=MESH
        )

    def to_grp(src, dst, ss, rs, there):
        return pltpu.make_async_remote_copy(
            src_ref=src, dst_ref=dst, send_sem=ss, recv_sem=rs, device_id={"grp": there}, device_id_type=MESH
        )

    loads = []
    for k, (src, dst) in enumerate(
        ((h_hbm, h), (g_hbm, g), (nbr_hbm, nbr), (msk_hbm, msk), (cnbr_hbm, cnbr), (cmsk_hbm, cmsk))
    ):
        loads.append(pltpu.make_async_copy(src, dst, load_s.at[k]))
        loads[-1].start()

    plane = n_sub // 2
    line = lax.rem(si, 2)
    yz = si // 2

    def in_plane(d):
        there = lax.rem(yz + d, plane)
        return there, there * 2 + line

    def weights_scatter(array, received, ss, rs):
        size = array.shape[0] // plane

        def body(d, carry):
            chunk, there = in_plane(d)
            to_sub(array.at[rows_at(chunk * size, size)], received.at[rows_at((d - 1) * size, size)], ss, rs, there).start()
            return carry

        lax.fori_loop(1, plane, body, 0)

    def weights_line(array, received, lines, ss, rs, line_ss, line_rs):
        size = array.shape[0] // plane
        to_sub(received, received, ss, rs, above).wait_recv()

        def body(d, total):
            return total + received[rows_at((d - 1) * size, size), :].astype(F32)

        total = lax.fori_loop(1, plane, body, array[rows_at(yz * size, size), :].astype(F32))
        groups = lines.shape[0] // 2
        mine = line * groups + (gi if groups > 1 else 0)
        lines[mine] = total.astype(BF)
        copies = []
        for k in range(1, 2 * groups):
            sub_there = si if k < groups else si + 1 - 2 * line
            grp_there = lax.rem(gi + k, n_grp) if groups > 1 else gi
            copies.append(
                pltpu.make_async_remote_copy(
                    src_ref=lines.at[mine], dst_ref=lines.at[mine], send_sem=line_ss.at[k - 1], recv_sem=line_rs.at[k - 1],
                    device_id={"grp": grp_there, "sub": sub_there}, device_id_type=MESH,
                )
            )
            copies[-1].start()
        return copies

    def weights_gather(array, lines, copies, ss, rs):
        size = array.shape[0] // plane
        for c in copies:
            c.wait_recv()
        total = lines[0].astype(F32)
        for k in range(1, lines.shape[0]):
            total = total + lines[k].astype(F32)
        mine = rows_at(yz * size, size)
        array[mine, :] = total.astype(BF)

        def body(d, carry):
            to_sub(array.at[mine], array.at[mine], ss, rs, in_plane(d)[1]).start()
            return carry

        lax.fori_loop(1, plane, body, 0)

    barrier = pltpu.get_barrier_semaphore()

    def greet(sub_there, grp_there):
        pl.semaphore_signal(barrier, inc=1, device_id={"grp": grp_there, "sub": sub_there}, device_id_type=MESH)

    def greet_plane(d, carry):
        greet(in_plane(d)[1], gi)
        return carry

    lax.fori_loop(1, plane, greet_plane, 0)
    for k in range(1, 2 * n_grp):
        greet(si if k < n_grp else si + 1 - 2 * line, lax.rem(gi + k, n_grp))
    for there in (above, below):
        greet(there, gi)
        greet(there, sibling)

    def widen(i, carry):
        upd[rows_at(i * TILE, TILE), :] = h[rows_at(i * TILE, TILE), :].astype(F32)
        return carry

    loads[0].wait()
    lax.fori_loop(0, tiles, widen, 0)
    gather_rows(shi_s, upd, rowbuf, 0, halo_rows)
    gather_rows(slo_s, upd, rowbuf, halo_rows, halo_rows)
    stage[...] = rowbuf[0 : 2 * halo_rows, :].astype(BF)
    pl.semaphore_wait(barrier, plane - 1 + 2 * n_grp - 1 + 4)
    half = halo_rows // 2
    halo_copies = []
    for c in range(4):
        part = pl.ds(c * half, half)
        halo_copies.append(
            to_sub(stage.at[part], halo_in.at[part], halo_ss.at[c], halo_rs.at[c], above if c < 2 else below)
        )
        halo_copies[-1].start()

    loads[1].wait()
    acc[...] = jnp.zeros_like(acc)
    hist[...] = jnp.zeros_like(hist)

    def owners(i, carry):
        high, low = [], []
        for l in range(TILE // 128):
            v = owner[pl.ds(i * (TILE // 128) + l, 1), :]
            for t in range(crows // 256):
                st[i, t * 256 : (t + 1) * 256, l * 128 : (l + 1) * 128] = group_hot(v, t)
            high.append(one_hot((v >> 7).astype(F32), 16))
            low.append(one_hot((v & 127).astype(F32), 128))
        hist[...] += dot(jnp.concatenate(high, axis=1), jnp.concatenate(low, axis=1), 1, 1)
        acc[...] += dot(st[i], g[rows_at(i * TILE, TILE), :])
        return carry

    lax.fori_loop(0, tiles, owners, 0)
    hist_copies = []
    for d in range(1, n_grp):
        hist_copies.append(
            to_grp(hist, hist_in.at[d - 1], hist_ss.at[d - 1], hist_rs.at[d - 1], lax.rem(gi + d, n_grp))
        )
        hist_copies[-1].start()

    part_rows = crows // 2
    mine = rows_at(core * part_rows, part_rows)
    theirs = rows_at((1 - core) * part_rows, part_rows)

    def group_first(sums, send, received, ss, rs):
        send[...] = sums[theirs, :].astype(BF)
        copy = to_grp(send, received, ss.at[0], rs.at[0], sibling)
        copy.start()
        return [copy]

    def group_second(copies, sums, received, chip, other, ss, rs):
        copies[0].wait_recv()
        chip[...] = (sums[mine, :] + received[...].astype(F32)).astype(BF)
        copies.append(to_grp(chip, other, ss.at[1], rs.at[1], other_chip))
        copies[1].start()

    def group_third(copies, chip, other, scale, whole, ss, rs):
        copies[1].wait_recv()
        total = chip[...].astype(F32) + other[...].astype(F32)
        whole[mine, :] = (total if scale is None else total * scale[mine, :]).astype(BF)
        copies.append(to_grp(whole.at[mine], whole.at[mine], ss.at[2], rs.at[2], sibling))
        copies[2].start()

    g_copies = group_first(acc, gsend, gcore, gs_ss, gs_rs)

    for c in loads[2:]:
        c.wait()
    prepare_slots(nbr, msk, cidx, rows, halo_rows, hblocks)
    both_f = jnp.concatenate([wfs[...] * 0.5, wfo[...] * 0.5], axis=1)

    def dense(i, carry):
        part = rows_at(i * TILE, TILE)
        r = dot(h[part, :], both_f)
        own[part, :] = r[:, :D].astype(BF)
        far[part, :] = r[:, D:].astype(BF)
        return carry

    lax.fori_loop(0, tiles, dense, 0)
    build_selectors(cidx, sel, blocks)

    group_second(g_copies, acc, gcore, gchip, gx, gs_ss, gs_rs)

    for c in halo_copies:
        c.wait_recv()
    halo[0:halo_rows, :] = (halo_in[0:halo_rows, :].astype(F32) * has_below).astype(BF)
    halo[halo_rows:, :] = (halo_in[halo_rows:, :].astype(F32) * has_above).astype(BF)
    farh[...] = dot(halo[...], wfo[...] * 0.5).astype(BF)

    acc[...] = jnp.zeros_like(acc)

    def forward_edges(i):
        for u in range(TILE // BLK):
            b = i * (TILE // BLK) + u
            hb = b & (hblocks - 1)
            window = jnp.concatenate(
                [
                    far[rows_at(b * BLK, BLK), :],
                    farh[rows_at(hb * BLK, BLK), :],
                    farh[rows_at(halo_rows + hb * BLK, BLK), :],
                    own[rows_at(b * BLK, BLK), :],
                ],
                axis=0,
            )
            total, q = edge_forward(sel[b], window)
            slope[b] = q
            summed[rows_at(b * BLK, BLK), :] = total.astype(BF)

    def forward_new(i):
        part = rows_at(i * TILE, TILE)
        new = h[part, :].astype(F32) + dot(summed[part, :], wfn[...])
        upd[part, :] = new
        return new.astype(BF)

    def forward_update(i):
        acc[...] += dot(st[i], forward_new(i))

    def forward_tiles(p, carry):
        forward_update(p * 2 - 2)
        forward_update(p * 2 - 1)
        forward_edges(p * 2)
        forward_edges(p * 2 + 1)
        return carry

    forward_edges(0)
    forward_edges(1)
    lax.fori_loop(1, tiles // 2, forward_tiles, 0)
    new_a, new_b = forward_new(tiles - 2), forward_new(tiles - 1)
    acc[theirs, :] += dot(st[tiles - 2, theirs, :], new_a) + dot(st[tiles - 1, theirs, :], new_b)

    t_copies = group_first(acc, tsend, tcore, ts_ss, ts_rs)
    acc[mine, :] += dot(st[tiles - 2, mine, :], new_a) + dot(st[tiles - 1, mine, :], new_b)
    group_third(g_copies, gchip, gx, None, gall, gs_ss, gs_rs)
    for c in hist_copies:
        c.wait_recv()
    counts = hist[...]
    for d in range(1, n_grp):
        counts = counts + hist_in[d - 1]
    for k in range(crows // 128):
        rcnt[k * 128 : (k + 1) * 128, :] = 1.0 / jnp.maximum(
            jnp.transpose(jnp.broadcast_to(counts[k : k + 1], (128, 128))), 1.0
        )
    prepare_slots(cnbr, cmsk, ccidx, crows, chalo_rows, 1)
    g_copies[2].wait_recv()
    yc[...] = dot(gall[...], wpr[...], 1, 1)
    group_second(t_copies, acc, tcore, tchip, tx, ts_ss, ts_rs)
    dsc[...] = (dot(yc[...].astype(BF), wcn[...], 1, 1) * 0.5).astype(BF)
    build_selectors(ccidx, csel, cblocks)
    group_third(t_copies, tchip, tx, rcnt, cin, ts_ss, ts_rs)
    cinf[mine, :] = cin[mine, :].astype(F32)
    cinf[theirs, :] = jnp.zeros((part_rows, D), F32)
    gather_rows(cshi_s, cinf, cstaged, 0, chalo_rows)
    gather_rows(cslo_s, cinf, cstaged, chalo_rows, chalo_rows)
    cstage[...] = cstaged[...].astype(BF)
    ch_copies = []
    for c in range(4):
        part = pl.ds((c // 2) * chalo_rows, chalo_rows)
        ch_copies.append(
            pltpu.make_async_remote_copy(
                src_ref=cstage.at[part], dst_ref=chalo_in.at[c % 2, part], send_sem=ch_ss.at[c], recv_sem=ch_rs.at[c],
                device_id={"grp": (gi, sibling)[c % 2], "sub": (above, below)[c // 2]}, device_id_type=MESH,
            )
        )
        ch_copies[-1].start()
    t_copies[2].wait_recv()
    r = dot(cin[...], jnp.concatenate([wcs[...] * 0.5, wco[...] * 0.5], axis=1))
    cown[...] = r[:, :D].astype(BF)
    cfar[...] = r[:, D:].astype(BF)

    def known_part(i, carry):
        part = rows_at(i * TILE, TILE)
        gw[part, :] = dot(g[part, :], wfn[...], 1, 1) * 0.5
        return carry

    lax.fori_loop(0, tiles, known_part, 0)
    for c in ch_copies:
        c.wait_recv()
    arrived = chalo_in[0].astype(F32) + chalo_in[1].astype(F32)
    chalo[0:chalo_rows, :] = (arrived[0:chalo_rows] * has_below).astype(BF)
    chalo[chalo_rows:, :] = (arrived[chalo_rows:] * has_above).astype(BF)
    cfarh[...] = dot(chalo[...], wco[...] * 0.5).astype(BF)
    chacc[...] = jnp.zeros_like(chacc)

    def mid_blocks(p, carry):
        both = None
        for u in range(16):
            b = p * 16 + u
            part = rows_at(b * BLK, BLK)
            total, q = edge_forward(csel[b], jnp.concatenate([cfar[part, :], cfarh[...], cown[part, :]], axis=0))
            csum[part, :] = total.astype(BF)
            grads = edge_backward(csel[b], q, dsc[part, :])
            cdfar[part, :] = grads[0:BLK]
            both = grads[BLK : 3 * BLK] if both is None else both + grads[BLK : 3 * BLK]
            cdown[part, :] = grads[3 * BLK :].astype(BF)
        chacc[...] += both
        return carry

    lax.fori_loop(0, cblocks // 16, mid_blocks, 0)
    cback[...] = chacc[...].astype(BF)
    cb_copies = []
    for c in range(2):
        part = pl.ds(c * chalo_rows, chalo_rows)
        cb_copies.append(to_sub(cback.at[part], cback_in.at[part], cb_ss.at[c], cb_rs.at[c], (below, above)[c]))
        cb_copies[-1].start()

    cout[...] = (cin[...].astype(F32) + dot(csum[...], wcn[...])).astype(BF)
    cprol[...] = dot(cout[...], wpr[...]).astype(BF)

    r = dot(cin[...], jnp.concatenate([cdown[...], cdfar[...].astype(BF)], axis=1), 0, 0)
    w_e[0:128, :] = r[:, :D].astype(BF)
    w_e[128:256, :] = (r[:, D:] + dot(chalo[...], cback[...], 0, 0)).astype(BF)
    w_e[256:384, :] = dot(csum[...], yc[...].astype(BF), 0, 0).astype(BF)
    w_e[384:512, :] = dot(cout[...], gall[...], 0, 0).astype(BF)
    weights_scatter(w_e, rs_e, e_ss, e_rs)

    def prolonged(p, carry):
        for u in range(4):
            i = p * 4 + u
            part = rows_at(i * TILE, TILE)
            result[part, :] = (upd[part, :] + dot(st[i], cprol[...], 0, 0)).astype(BF)
        return carry

    lax.fori_loop(0, tiles // 4, prolonged, 0)
    stores = [pltpu.make_async_copy(result, result_hbm, store_s.at[0])]
    stores[0].start()
    for c in cb_copies:
        c.wait_recv()
    from_above = (cback_in[0:chalo_rows, :].astype(F32) * has_above).astype(BF)
    from_below = (cback_in[chalo_rows:, :].astype(F32) * has_below).astype(BF)
    for t in range(crows // 256):
        part = slice(t * 256, (t + 1) * 256)
        cdfar[part, :] += dot(group_hot(cshi_v[...], t), from_above) + dot(group_hot(cslo_v[...], t), from_below)
    dcin = yc[...] + dot(cdown[...], wcs[...], 1, 1) + dot(cdfar[...].astype(BF), wco[...], 1, 1)
    m = (dcin * rcnt[...]).astype(BF)
    mm[:, :D] = m
    mm[:, D:] = (dot(m, wfn[...], 1, 1) * 0.5).astype(BF)

    sum_f[...] = jnp.zeros_like(sum_f)

    def cotangents(p, carry):
        for u in range(4):
            i = p * 4 + u
            part = rows_at(i * TILE, TILE)
            r = dot(st[i], mm[...], 0, 0)
            y = g[part, :].astype(F32) + r[:, :D]
            upd[part, :] = y
            dsum[part, :] = (gw[part, :] + r[:, D:]).astype(BF)
        return carry

    lax.fori_loop(0, tiles // 4, cotangents, 0)

    e_copies = weights_line(w_e, rs_e, line_e, e_ss, e_rs, el_ss, el_rs)

    bk_copies = []
    for c in range(2 * hblocks):
        part = pl.ds(c * BLK, BLK)
        bk_copies.append(
            to_sub(back.at[part], back_in.at[part], bk_ss.at[c], bk_rs.at[c], below if c < hblocks else above)
        )

    def backward_edges(hb):
        both = None
        for u in range(blocks // hblocks):
            b = u * hblocks + hb
            part = rows_at(b * BLK, BLK)
            grads = edge_backward(sel[b], slope[b], dsum[part, :])
            dfar[part, :] = grads[0:BLK].astype(BF)
            down[part, :] = grads[3 * BLK :].astype(BF)
            both = grads[BLK : 3 * BLK] if both is None else both + grads[BLK : 3 * BLK]
        back[rows_at(hb * BLK, BLK), :] = both[0:BLK].astype(BF)
        back[rows_at(halo_rows + hb * BLK, BLK), :] = both[BLK:].astype(BF)
        for c, there in ((hb, below), (hblocks + hb, above)):
            part = rows_at(c * BLK, BLK)
            to_sub(back.at[part], back_in.at[part], bk_ss.at[c], bk_rs.at[c], there).start()

    def backward_weights(hb):
        parts = [rows_at((u * hblocks + hb) * BLK, BLK) for u in range(blocks // hblocks)]
        grads = jnp.concatenate([jnp.concatenate([down[p, :], dfar[p, :]], axis=1) for p in parts], axis=0)
        r = dot(jnp.concatenate([h[p, :] for p in parts], axis=0), grads, 0, 0)
        below_part = rows_at(hb * BLK, BLK)
        above_part = rows_at(halo_rows + hb * BLK, BLK)
        halo_grad = jnp.concatenate([back[below_part, :], back[above_part, :]], axis=0)
        halo_row = jnp.concatenate([halo[below_part, :], halo[above_part, :]], axis=0)
        sum_f[0:128, :] += r[:, :D]
        sum_f[128:256, :] += r[:, D:] + dot(halo_row, halo_grad, 0, 0)
        y = jnp.concatenate([upd[p, :] for p in parts], axis=0)
        sum_f[256:384, :] += dot(jnp.concatenate([summed[p, :] for p in parts], axis=0), y.astype(BF), 0, 0)
        return parts, grads, y

    def backward_latents(parts, grads, y):
        r = dot(grads, jnp.concatenate([wfs[...], wfo[...]], axis=1), 1, 1) + y
        for u, p in enumerate(parts):
            upd[p, :] = r[u * BLK : (u + 1) * BLK]

    def backward_step(hb, carry):
        backward_latents(*backward_weights(hb - 1))
        backward_edges(hb)
        return carry

    backward_edges(0)
    lax.fori_loop(1, hblocks, backward_step, 0)
    last = backward_weights(hblocks - 1)
    w_f[...] = sum_f[...].astype(BF)
    weights_scatter(w_f, rs_f, f_ss, f_rs)
    weights_gather(all_e, line_e, e_copies, ea_ss, ea_rs)
    backward_latents(*last)


    f_copies = weights_line(w_f, rs_f, line_f, f_ss, f_rs, fl_ss, fl_rs)

    for c in bk_copies:
        c.wait_recv()
    halo[0:halo_rows, :] = (dot(back_in[0:halo_rows, :], wfo[...], 1, 1) * has_above).astype(BF)
    halo[halo_rows:, :] = (dot(back_in[halo_rows:, :], wfo[...], 1, 1) * has_below).astype(BF)
    group = 1024

    def returned(i, carry):
        part = rows_at(i * group, group)
        hots = []
        for t in range(group // 256):
            row = []
            for table in (shi_v, slo_v):
                for l in range(halo_rows // 128):
                    row.append(group_hot(table[l : l + 1, :], i * (group // 256) + t))
            hots.append(jnp.concatenate(row, axis=1))
        grad_h[part, :] = (upd[part, :] + dot(jnp.concatenate(hots, axis=0), halo[...])).astype(BF)
        return carry

    def store_half(k):
        part = pl.ds(k * (rows // 2), rows // 2)
        stores.append(pltpu.make_async_copy(grad_h.at[part], grad_h_hbm.at[part], store_s.at[1 + k]))
        stores[-1].start()

    lax.fori_loop(0, rows // group // 2, returned, 0)
    store_half(0)
    weights_gather(all_f, line_f, f_copies, fa_ss, fa_rs)
    lax.fori_loop(rows // group // 2, rows // group, returned, 0)
    store_half(1)

    def finish(array, ss, rs, first, count, sem):
        size = array.shape[0] // plane
        others = array.at[pl.ds(0, array.shape[0] - size)]
        to_sub(others, others, ss, rs, above).wait_recv()
        stores.append(
            pltpu.make_async_copy(array.at[pl.ds(0, count * D)], grad_w_hbm.at[pl.ds(first * D, count * D)], sem)
        )
        stores[-1].start()

    finish(all_e, ea_ss, ea_rs, 3, 4, store_s.at[3])
    finish(all_f, fa_ss, fa_rs, 0, 3, store_s.at[4])

    for c in halo_copies + hist_copies + g_copies + t_copies + ch_copies + cb_copies:
        c.wait_send()
    for c in bk_copies + f_copies + e_copies:
        c.wait_send()
    for c in stores:
        c.wait()
    for received, array, ss, gather_ss, rs in ((rs_e, all_e, e_ss, ea_ss, e_rs), (rs_f, all_f, f_ss, fa_ss, f_rs)):
        to_sub(received, received, ss, rs, above).wait_send()
        others = array.at[pl.ds(0, array.shape[0] - array.shape[0] // plane)]
        to_sub(others, others, gather_ss, rs, above).wait_send()


def step(
    n_grp, n_sub,
    states, cotangent, fine_self, fine_other, fine_node, coarse_self, coarse_other, coarse_node, prolong,
    fine_nbr, fine_mask, fine_send_lo, fine_send_hi, coarse_nbr, coarse_mask, coarse_send_lo, coarse_send_hi, coarse_owner,
):
    rows, slots = fine_nbr.shape
    crows = coarse_nbr.shape[0]
    halo = fine_send_lo.shape[0]
    chalo = coarse_send_lo.shape[0]
    blocks, cblocks = rows // BLK, crows // BLK
    edges = BLK * slots
    vmem = pl.BlockSpec(memory_space=pltpu.VMEM)
    smem = pl.BlockSpec(memory_space=pltpu.SMEM)
    hbm = pl.BlockSpec(memory_space=pl.ANY)
    V = pltpu.VMEM
    dma = pltpu.SemaphoreType.DMA
    w_rows = 4 * D
    wc = w_rows // (n_sub // 2)
    i32 = jnp.int32
    scratch = [
        V((rows, D), BF), V((rows, D), BF), V((slots, rows), i32), V((slots, rows), i32),
        V((slots, crows), i32), V((slots, crows), i32), V((rows, D), BF), V((rows, D), BF),
        V((2 * halo, D), BF), V((2 * halo, D), BF), V((2 * halo, D), BF),
        V((rows, D), BF), V((2 * halo, D), BF), V((rows, D), BF),
        V((blocks, 8, 128), F32), V((blocks, 4 * BLK, edges), BF), V((blocks, edges, D), BF),
        V((rows // TILE, crows, TILE), BF),
        V((rows, D), BF), V((rows, D), BF), V((rows, D), F32), V((rows, D), F32), V((crows, D), F32),
        V((16, 128), F32), V((n_grp - 1, 16, 128), F32), V((crows, D), F32),
        V((crows // 2, D), BF), V((crows // 2, D), BF), V((crows // 2, D), BF), V((crows // 2, D), BF), V((crows, D), BF),
        V((crows // 2, D), BF), V((crows // 2, D), BF), V((crows // 2, D), BF), V((crows // 2, D), BF), V((crows, D), BF),
        V((crows, D), F32), V((2 * chalo, D), F32), V((2 * chalo, D), BF), V((2, 2 * chalo, D), BF), V((2 * chalo, D), BF),
        V((crows, D), BF), V((crows, D), BF), V((2 * chalo, D), BF),
        V((cblocks, 8, 128), F32), V((cblocks, 4 * BLK, edges), BF),
        V((crows, D), F32), V((crows, D), BF), V((crows, D), BF), V((crows, D), BF), V((crows, D), F32),
        V((2 * chalo, D), F32), V((2 * chalo, D), BF), V((2 * chalo, D), BF),
        V((crows, D), BF), V((crows, D), BF), V((crows, 2 * D), BF),
        V((2 * halo, D), BF), V((2 * halo, D), BF),
        V((w_rows, D), BF), V((w_rows - wc, D), BF), V((2, wc, D), BF), V((w_rows, D), BF),
        V((w_rows, D), BF), V((w_rows, D), F32), V((w_rows - wc, D), BF), V((2 * n_grp, wc, D), BF), V((w_rows, D), BF),
        dma((6,)), dma((5,)), dma((4,)), dma((4,)),
        dma((n_grp - 1,)), dma((n_grp - 1,)), dma((3,)), dma((3,)), dma((3,)), dma((3,)),
        dma((4,)), dma((4,)), dma((2,)), dma((2,)),
        dma((2 * halo // BLK,)), dma((2 * halo // BLK,)),
        dma, dma, dma((1,)), dma((1,)), dma, dma,
        dma, dma, dma((2 * n_grp - 1,)), dma((2 * n_grp - 1,)), dma, dma,
    ]
    outs = pl.pallas_call(
        functools.partial(kernel, n_grp, n_sub),
        out_shape=(
            jax.ShapeDtypeStruct((rows, D), BF),
            jax.ShapeDtypeStruct((rows, D), BF),
            jax.ShapeDtypeStruct((7 * D, D), BF),
        ),
        in_specs=[hbm] * 2 + [vmem] * 7 + [hbm] * 4 + [smem] * 4 + [vmem] * 5,
        out_specs=(hbm, hbm, hbm),
        scratch_shapes=scratch,
        compiler_params=pltpu.CompilerParams(
            collective_id=0, has_side_effects=True, vmem_limit_bytes=60 * 1024 * 1024 + 512 * 1024
        ),
    )(
        states, cotangent, fine_self, fine_other, fine_node, coarse_self, coarse_other, coarse_node, prolong,
        fine_nbr.T, fine_mask.T, coarse_nbr.T, coarse_mask.T,
        fine_send_lo, fine_send_hi, coarse_send_lo, coarse_send_hi,
        fine_send_lo.reshape(-1, 128), fine_send_hi.reshape(-1, 128),
        coarse_send_lo.reshape(1, -1), coarse_send_hi.reshape(1, -1),
        coarse_owner.reshape(-1, 128),
    )
    return copied((outs[0], outs[1], outs[2].reshape(7, D, D)), 2)


def solution(mesh):
    rows2 = P(("grp", "sub"), None)
    rows1 = P(("grp", "sub"))
    in_specs = (
        (rows2, rows2) + (P(),) * 7
        + (rows2, rows2, rows1, rows1)
        + (P("sub", None), P("sub", None), P("sub"), P("sub"), rows1)
    )
    return jax.shard_map(
        functools.partial(step, mesh.shape["grp"], mesh.shape["sub"]),
        mesh=mesh, in_specs=in_specs, out_specs=(rows2, rows2, P()), check_vma=False,
    )
```

```python
import functools

import jax
import jax.numpy as jnp
from jax import lax
from jax.experimental import pallas as pl
from jax.experimental.pallas import tpu as pltpu
from jax.sharding import PartitionSpec as P

MESH = pl.DeviceIdType.MESH
BF = jnp.bfloat16
F32 = jnp.float32
D = 128
BLK = 64
TILE = 512


def dot(a, b, ca=1, cb=0):
    return lax.dot_general(a, b, (((ca,), (cb,)), ((), ())), preferred_element_type=F32)


def rows_at(start, size):
    if isinstance(start, int):
        return pl.ds(start, size)
    return pl.ds(pl.multiple_of(start, size if size % 8 == 0 else 8), size)


def spread(row, rows):
    one = jnp.broadcast_to(row, (16, row.shape[1])).astype(BF)
    return jnp.concatenate([one] * (rows // 16), axis=0)


def iota_bf(rows, lanes, base=0):
    return (lax.broadcasted_iota(jnp.int32, (rows, lanes), 0) + base).astype(F32).astype(BF)


def one_hot(row, rows, base=0):
    hit = iota_bf(rows, row.shape[1], base) == spread(row, rows)
    return jnp.where(hit, jnp.ones((), BF), jnp.zeros((), BF))


def group_hot(values, group):
    inside = jnp.where((values >> 8) == group, values & 255, -1).astype(F32)
    return one_hot(inside, 256)


def prepare_slots(nbr, msk, cidx, rows, halo, halo_blocks):
    def body(p, carry):
        v = nbr[:, rows_at(p * 128, 128)]
        used = msk[:, rows_at(p * 128, 128)] > 0
        lane = lax.broadcasted_iota(jnp.int32, (8, 128), 1)
        slot = lax.broadcasted_iota(jnp.int32, (8, 128), 0)
        blk = 2 * p + (lane >> 6)
        hblk = blk & (halo_blocks - 1)
        col = jnp.where(
            v < rows,
            v - blk * BLK,
            jnp.where(v < rows + halo, v - rows - hblk * BLK + BLK, v - rows - halo - hblk * BLK + 2 * BLK),
        )
        col = jnp.where(used, col, -1)
        own = jnp.where(used, 3 * BLK + (lane & (BLK - 1)), -1)
        first = lane < BLK

        def halves(x):
            later = pltpu.roll(x, 4, 0)
            return (
                jnp.where(first, x, pltpu.roll(later, BLK, 1)),
                jnp.where(first, pltpu.roll(x, BLK, 1), later),
            )

        for half, (c, o) in enumerate(zip(halves(col), halves(own))):
            cidx[2 * p + half] = jnp.where(slot < 4, c, pltpu.roll(o, 4, 0)).astype(F32)
        return carry

    lax.fori_loop(0, rows // 128, body, 0)


def build_selectors(cidx, sel, blocks):
    def body(p, carry):
        for u in range(4):
            b = p * 4 + u
            idx = cidx[b]
            for j in range(4):
                sel[b, 0 : 3 * BLK, j * 128 : (j + 1) * 128] = one_hot(idx[j : j + 1], 3 * BLK)
                sel[b, 3 * BLK : 4 * BLK, j * 128 : (j + 1) * 128] = one_hot(idx[4 + j : 5 + j], BLK, 3 * BLK)
        return carry

    lax.fori_loop(0, blocks // 4, body, 0)


def gather_rows(index, source, staged, start, count):
    def body(i, carry):
        at = pl.multiple_of(start + i * 16, 16)
        for u in range(16):
            staged[pl.ds(at + u, 1), :] = source[pl.ds(index[i * 16 + u], 1), :]
        return carry

    lax.fori_loop(0, count // 16, body, 0)


def edge_forward(sel, window):
    half = dot(sel, window, 0, 0)
    up = 1.0 + jnp.tanh(half)
    act = half * up
    slope = (up + act * (2.0 - up)).astype(BF)
    total = act[0:BLK]
    for k in range(1, 8):
        total = total + act[k * BLK : (k + 1) * BLK]
    return total, slope


def edge_backward(sel, slope, half_grad):
    grad = jnp.concatenate([half_grad] * 8, axis=0) * slope
    return dot(sel, grad)


def copy_kernel(*refs):
    count = len(refs) // 2
    for k in range(count):
        refs[count + k][...] = refs[k][...].astype(refs[count + k].dtype)


def copied(arrays, steps):
    specs = []
    for a in arrays:
        if a.ndim == 2:
            specs.append(pl.BlockSpec((a.shape[0] // steps, a.shape[1]), lambda i: (i, 0)))
        else:
            specs.append(pl.BlockSpec((a.shape[0], a.shape[1] // steps, a.shape[2]), lambda i: (0, i, 0)))
    return pl.pallas_call(
        copy_kernel,
        grid=(steps,),
        out_shape=tuple(jax.ShapeDtypeStruct(a.shape, BF if a.ndim == 2 else F32) for a in arrays),
        in_specs=specs,
        out_specs=tuple(specs),
    )(*arrays)


def kernel(
    n_grp, n_sub,
    h_hbm, g_hbm, wfs, wfo, wfn, wcs, wco, wcn, wpr, nbr_hbm, msk_hbm, cnbr_hbm, cmsk_hbm,
    slo_s, shi_s, cslo_s, cshi_s, slo_v, shi_v, cslo_v, cshi_v, owner,
    result_hbm, grad_h_hbm, grad_w_hbm,
    h, g, nbr, msk, cnbr, cmsk, result, grad_h,
    stage, halo_in, halo, far_dfar, farh, own_dsum, cidx, sel, slope, st, summed, down, upd, rowbuf, acc,
    hist, hist_in, rcnt, gsend, gcore, gchip, gx, gall, tsend, tcore, tchip, tx, cin, cinf, cstaged, cstage, chalo_in, chalo, cown, cfar, cfarh,
    ccidx, csel, yc, dsc, csum, cdown, cdfar, chacc, cback, cback_in, cout, cprol, mm, back, back_in,
    w_e, rs_e, line_e, all_e, w_f, sum_f, rs_f, line_f, all_f,
    load_s, store_s, halo_ss, halo_rs, hist_ss, hist_rs, gs_ss, gs_rs, ts_ss, ts_rs,
    ch_ss, ch_rs, cb_ss, cb_rs, bk_ss, bk_rs, e_ss, e_rs, el_ss, el_rs, ea_ss, ea_rs, f_ss, f_rs, fl_ss, fl_rs, fa_ss, fa_rs,
):
    own, dsum = own_dsum, own_dsum
    far, dfar = far_dfar, far_dfar
    gw = rowbuf
    rows = h.shape[0]
    crows = cnbr.shape[1]
    halo_rows = shi_s.shape[0]
    chalo_rows = cshi_s.shape[0]
    tiles = rows // TILE
    blocks = rows // BLK
    cblocks = crows // BLK
    hblocks = halo_rows // BLK
    gi = lax.axis_index("grp")
    si = lax.axis_index("sub")
    above = lax.rem(si + 1, n_sub)
    below = lax.rem(si + n_sub - 1, n_sub)
    core = lax.rem(gi, 2)
    sibling = gi + 1 - 2 * core
    other_chip = lax.rem(gi + 2, n_grp)
    has_below = jnp.where(si > 0, 1.0, 0.0).astype(F32)
    has_above = jnp.where(si < n_sub - 1, 1.0, 0.0).astype(F32)

    def to_sub(src, dst, ss, rs, there):
        return pltpu.make_async_remote_copy(
            src_ref=src, dst_ref=dst, send_sem=ss, recv_sem=rs, device_id={"sub": there}, device_id_type=MESH
        )

    def to_grp(src, dst, ss, rs, there):
        return pltpu.make_async_remote_copy(
            src_ref=src, dst_ref=dst, send_sem=ss, recv_sem=rs, device_id={"grp": there}, device_id_type=MESH
        )

    loads = []
    for k, (src, dst) in enumerate(
        ((h_hbm, h), (g_hbm, g), (nbr_hbm, nbr), (msk_hbm, msk), (cnbr_hbm, cnbr), (cmsk_hbm, cmsk))
    ):
        loads.append(pltpu.make_async_copy(src, dst, load_s.at[k]))
        loads[-1].start()

    plane = n_sub // 2
    line = lax.rem(si, 2)
    yz = si // 2

    def in_plane(d):
        there = lax.rem(yz + d, plane)
        return there, there * 2 + line

    def weights_scatter(array, received, ss, rs):
        size = array.shape[0] // plane

        def body(d, carry):
            chunk, there = in_plane(d)
            to_sub(array.at[rows_at(chunk * size, size)], received.at[rows_at((d - 1) * size, size)], ss, rs, there).start()
            return carry

        lax.fori_loop(1, plane, body, 0)

    def weights_line(array, received, lines, ss, rs, line_ss, line_rs):
        size = array.shape[0] // plane
        to_sub(received, received, ss, rs, above).wait_recv()

        def body(d, total):
            return total + received[rows_at((d - 1) * size, size), :].astype(F32)

        total = lax.fori_loop(1, plane, body, array[rows_at(yz * size, size), :].astype(F32))
        groups = lines.shape[0] // 2
        mine = line * groups + (gi if groups > 1 else 0)
        lines[mine] = total.astype(BF)
        copies = []
        for k in range(1, 2 * groups):
            sub_there = si if k < groups else si + 1 - 2 * line
            grp_there = lax.rem(gi + k, n_grp) if groups > 1 else gi
            copies.append(
                pltpu.make_async_remote_copy(
                    src_ref=lines.at[mine], dst_ref=lines.at[mine], send_sem=line_ss.at[k - 1], recv_sem=line_rs.at[k - 1],
                    device_id={"grp": grp_there, "sub": sub_there}, device_id_type=MESH,
                )
            )
            copies[-1].start()
        return copies

    def weights_gather(array, lines, copies, ss, rs):
        size = array.shape[0] // plane
        for c in copies:
            c.wait_recv()
        total = lines[0].astype(F32)
        for k in range(1, lines.shape[0]):
            total = total + lines[k].astype(F32)
        mine = rows_at(yz * size, size)
        array[mine, :] = total.astype(BF)

        def body(d, carry):
            to_sub(array.at[mine], array.at[mine], ss, rs, in_plane(d)[1]).start()
            return carry

        lax.fori_loop(1, plane, body, 0)

    barrier = pltpu.get_barrier_semaphore()

    def greet(sub_there, grp_there):
        pl.semaphore_signal(barrier, inc=1, device_id={"grp": grp_there, "sub": sub_there}, device_id_type=MESH)

    def greet_plane(d, carry):
        greet(in_plane(d)[1], gi)
        return carry

    lax.fori_loop(1, plane, greet_plane, 0)
    for k in range(1, 2 * n_grp):
        greet(si if k < n_grp else si + 1 - 2 * line, lax.rem(gi + k, n_grp))
    for there in (above, below):
        greet(there, gi)
        greet(there, sibling)

    def widen(i, carry):
        upd[rows_at(i * TILE, TILE), :] = h[rows_at(i * TILE, TILE), :].astype(F32)
        return carry

    loads[0].wait()
    lax.fori_loop(0, tiles, widen, 0)
    gather_rows(shi_s, upd, rowbuf, 0, halo_rows)
    gather_rows(slo_s, upd, rowbuf, halo_rows, halo_rows)
    stage[...] = rowbuf[0 : 2 * halo_rows, :].astype(BF)
    pl.semaphore_wait(barrier, plane - 1 + 2 * n_grp - 1 + 4)
    half = halo_rows // 2
    halo_copies = []
    for c in range(4):
        part = pl.ds(c * half, half)
        halo_copies.append(
            to_sub(stage.at[part], halo_in.at[part], halo_ss.at[c], halo_rs.at[c], above if c < 2 else below)
        )
        halo_copies[-1].start()

    loads[1].wait()
    acc[...] = jnp.zeros_like(acc)
    hist[...] = jnp.zeros_like(hist)

    def owners(i, carry):
        high, low = [], []
        for l in range(TILE // 128):
            v = owner[pl.ds(i * (TILE // 128) + l, 1), :]
            for t in range(crows // 256):
                st[i, t * 256 : (t + 1) * 256, l * 128 : (l + 1) * 128] = group_hot(v, t)
            high.append(one_hot((v >> 7).astype(F32), 16))
            low.append(one_hot((v & 127).astype(F32), 128))
        hist[...] += dot(jnp.concatenate(high, axis=1), jnp.concatenate(low, axis=1), 1, 1)
        acc[...] += dot(st[i], g[rows_at(i * TILE, TILE), :])
        return carry

    lax.fori_loop(0, tiles, owners, 0)
    hist_copies = []
    for d in range(1, n_grp):
        hist_copies.append(
            to_grp(hist, hist_in.at[d - 1], hist_ss.at[d - 1], hist_rs.at[d - 1], lax.rem(gi + d, n_grp))
        )
        hist_copies[-1].start()

    part_rows = crows // 2
    mine = rows_at(core * part_rows, part_rows)
    theirs = rows_at((1 - core) * part_rows, part_rows)

    def group_first(sums, send, received, ss, rs):
        send[...] = sums[theirs, :].astype(BF)
        copy = to_grp(send, received, ss.at[0], rs.at[0], sibling)
        copy.start()
        return [copy]

    def group_second(copies, sums, received, chip, other, ss, rs):
        copies[0].wait_recv()
        chip[...] = (sums[mine, :] + received[...].astype(F32)).astype(BF)
        copies.append(to_grp(chip, other, ss.at[1], rs.at[1], other_chip))
        copies[1].start()

    def group_third(copies, chip, other, scale, whole, ss, rs):
        copies[1].wait_recv()
        total = chip[...].astype(F32) + other[...].astype(F32)
        whole[mine, :] = (total if scale is None else total * scale[mine, :]).astype(BF)
        copies.append(to_grp(whole.at[mine], whole.at[mine], ss.at[2], rs.at[2], sibling))
        copies[2].start()

    g_copies = group_first(acc, gsend, gcore, gs_ss, gs_rs)

    for c in loads[2:]:
        c.wait()
    prepare_slots(nbr, msk, cidx, rows, halo_rows, hblocks)
    both_f = jnp.concatenate([wfs[...] * 0.5, wfo[...] * 0.5], axis=1)

    def dense(i, carry):
        part = rows_at(i * TILE, TILE)
        r = dot(h[part, :], both_f)
        own[part, :] = r[:, :D].astype(BF)
        far[part, :] = r[:, D:].astype(BF)
        return carry

    lax.fori_loop(0, tiles, dense, 0)
    build_selectors(cidx, sel, blocks)

    group_second(g_copies, acc, gcore, gchip, gx, gs_ss, gs_rs)

    for c in halo_copies:
        c.wait_recv()
    halo[0:halo_rows, :] = (halo_in[0:halo_rows, :].astype(F32) * has_below).astype(BF)
    halo[halo_rows:, :] = (halo_in[halo_rows:, :].astype(F32) * has_above).astype(BF)
    farh[...] = dot(halo[...], wfo[...] * 0.5).astype(BF)

    acc[...] = jnp.zeros_like(acc)

    def forward_edges(i):
        for u in range(TILE // BLK):
            b = i * (TILE // BLK) + u
            hb = b & (hblocks - 1)
            window = jnp.concatenate(
                [
                    far[rows_at(b * BLK, BLK), :],
                    farh[rows_at(hb * BLK, BLK), :],
                    farh[rows_at(halo_rows + hb * BLK, BLK), :],
                    own[rows_at(b * BLK, BLK), :],
                ],
                axis=0,
            )
            total, q = edge_forward(sel[b], window)
            slope[b] = q
            summed[rows_at(b * BLK, BLK), :] = total.astype(BF)

    def forward_new(i):
        part = rows_at(i * TILE, TILE)
        new = h[part, :].astype(F32) + dot(summed[part, :], wfn[...])
        upd[part, :] = new
        return new.astype(BF)

    def forward_update(i):
        acc[...] += dot(st[i], forward_new(i))

    def forward_tiles(p, carry):
        forward_update(p * 2 - 2)
        forward_update(p * 2 - 1)
        forward_edges(p * 2)
        forward_edges(p * 2 + 1)
        return carry

    forward_edges(0)
    forward_edges(1)
    lax.fori_loop(1, tiles // 2, forward_tiles, 0)
    new_a, new_b = forward_new(tiles - 2), forward_new(tiles - 1)
    acc[theirs, :] += dot(st[tiles - 2, theirs, :], new_a) + dot(st[tiles - 1, theirs, :], new_b)

    t_copies = group_first(acc, tsend, tcore, ts_ss, ts_rs)
    acc[mine, :] += dot(st[tiles - 2, mine, :], new_a) + dot(st[tiles - 1, mine, :], new_b)
    group_third(g_copies, gchip, gx, None, gall, gs_ss, gs_rs)
    group_second(t_copies, acc, tcore, tchip, tx, ts_ss, ts_rs)
    for c in hist_copies:
        c.wait_recv()
    counts = hist[...]
    for d in range(1, n_grp):
        counts = counts + hist_in[d - 1]
    for k in range(crows // 128):
        rcnt[k * 128 : (k + 1) * 128, :] = 1.0 / jnp.maximum(
            jnp.transpose(jnp.broadcast_to(counts[k : k + 1], (128, 128))), 1.0
        )
    prepare_slots(cnbr, cmsk, ccidx, crows, chalo_rows, 1)
    g_copies[2].wait_recv()
    yc[...] = dot(gall[...], wpr[...], 1, 1)
    dsc[...] = (dot(yc[...].astype(BF), wcn[...], 1, 1) * 0.5).astype(BF)
    build_selectors(ccidx, csel, cblocks)
    group_third(t_copies, tchip, tx, rcnt, cin, ts_ss, ts_rs)
    cinf[mine, :] = cin[mine, :].astype(F32)
    cinf[theirs, :] = jnp.zeros((part_rows, D), F32)
    gather_rows(cshi_s, cinf, cstaged, 0, chalo_rows)
    gather_rows(cslo_s, cinf, cstaged, chalo_rows, chalo_rows)
    cstage[...] = cstaged[...].astype(BF)
    ch_copies = []
    for c in range(4):
        part = pl.ds((c // 2) * chalo_rows, chalo_rows)
        ch_copies.append(
            pltpu.make_async_remote_copy(
                src_ref=cstage.at[part], dst_ref=chalo_in.at[c % 2, part], send_sem=ch_ss.at[c], recv_sem=ch_rs.at[c],
                device_id={"grp": (gi, sibling)[c % 2], "sub": (above, below)[c // 2]}, device_id_type=MESH,
            )
        )
        ch_copies[-1].start()
    t_copies[2].wait_recv()
    r = dot(cin[...], jnp.concatenate([wcs[...] * 0.5, wco[...] * 0.5], axis=1))
    cown[...] = r[:, :D].astype(BF)
    cfar[...] = r[:, D:].astype(BF)

    def known_part(i, carry):
        part = rows_at(i * TILE, TILE)
        gw[part, :] = dot(g[part, :], wfn[...], 1, 1) * 0.5
        return carry

    lax.fori_loop(0, tiles, known_part, 0)
    for c in ch_copies:
        c.wait_recv()
    arrived = chalo_in[0].astype(F32) + chalo_in[1].astype(F32)
    chalo[0:chalo_rows, :] = (arrived[0:chalo_rows] * has_below).astype(BF)
    chalo[chalo_rows:, :] = (arrived[chalo_rows:] * has_above).astype(BF)
    cfarh[...] = dot(chalo[...], wco[...] * 0.5).astype(BF)
    chacc[...] = jnp.zeros_like(chacc)

    def mid_blocks(p, carry):
        both = None
        for u in range(16):
            b = p * 16 + u
            part = rows_at(b * BLK, BLK)
            total, q = edge_forward(csel[b], jnp.concatenate([cfar[part, :], cfarh[...], cown[part, :]], axis=0))
            csum[part, :] = total.astype(BF)
            grads = edge_backward(csel[b], q, dsc[part, :])
            cdfar[part, :] = grads[0:BLK]
            both = grads[BLK : 3 * BLK] if both is None else both + grads[BLK : 3 * BLK]
            cdown[part, :] = grads[3 * BLK :].astype(BF)
        chacc[...] += both
        return carry

    lax.fori_loop(0, cblocks // 16, mid_blocks, 0)
    cback[...] = chacc[...].astype(BF)
    cb_copies = []
    for c in range(2):
        part = pl.ds(c * chalo_rows, chalo_rows)
        cb_copies.append(to_sub(cback.at[part], cback_in.at[part], cb_ss.at[c], cb_rs.at[c], (below, above)[c]))
        cb_copies[-1].start()

    cout[...] = (cin[...].astype(F32) + dot(csum[...], wcn[...])).astype(BF)
    cprol[...] = dot(cout[...], wpr[...]).astype(BF)

    r = dot(cin[...], jnp.concatenate([cdown[...], cdfar[...].astype(BF)], axis=1), 0, 0)
    w_e[0:128, :] = r[:, :D].astype(BF)
    w_e[128:256, :] = (r[:, D:] + dot(chalo[...], cback[...], 0, 0)).astype(BF)
    w_e[256:384, :] = dot(csum[...], yc[...].astype(BF), 0, 0).astype(BF)
    w_e[384:512, :] = dot(cout[...], gall[...], 0, 0).astype(BF)
    weights_scatter(w_e, rs_e, e_ss, e_rs)

    def prolonged(p, carry):
        for u in range(4):
            i = p * 4 + u
            part = rows_at(i * TILE, TILE)
            result[part, :] = (upd[part, :] + dot(st[i], cprol[...], 0, 0)).astype(BF)
        return carry

    lax.fori_loop(0, tiles // 4, prolonged, 0)
    stores = [pltpu.make_async_copy(result, result_hbm, store_s.at[0])]
    stores[0].start()
    for c in cb_copies:
        c.wait_recv()
    from_above = (cback_in[0:chalo_rows, :].astype(F32) * has_above).astype(BF)
    from_below = (cback_in[chalo_rows:, :].astype(F32) * has_below).astype(BF)
    for t in range(crows // 256):
        part = slice(t * 256, (t + 1) * 256)
        cdfar[part, :] += dot(group_hot(cshi_v[...], t), from_above) + dot(group_hot(cslo_v[...], t), from_below)
    dcin = yc[...] + dot(cdown[...], wcs[...], 1, 1) + dot(cdfar[...].astype(BF), wco[...], 1, 1)
    m = (dcin * rcnt[...]).astype(BF)
    mm[:, :D] = m
    mm[:, D:] = (dot(m, wfn[...], 1, 1) * 0.5).astype(BF)

    sum_f[...] = jnp.zeros_like(sum_f)

    def cotangents(p, carry):
        for u in range(4):
            i = p * 4 + u
            part = rows_at(i * TILE, TILE)
            r = dot(st[i], mm[...], 0, 0)
            y = g[part, :].astype(F32) + r[:, :D]
            upd[part, :] = y
            dsum[part, :] = (gw[part, :] + r[:, D:]).astype(BF)
        return carry

    lax.fori_loop(0, tiles // 4, cotangents, 0)

    e_copies = weights_line(w_e, rs_e, line_e, e_ss, e_rs, el_ss, el_rs)

    bk_copies = []
    for c in range(2 * hblocks):
        part = pl.ds(c * BLK, BLK)
        bk_copies.append(
            to_sub(back.at[part], back_in.at[part], bk_ss.at[c], bk_rs.at[c], below if c < hblocks else above)
        )

    def backward_edges(hb):
        both = None
        for u in range(blocks // hblocks):
            b = u * hblocks + hb
            part = rows_at(b * BLK, BLK)
            grads = edge_backward(sel[b], slope[b], dsum[part, :])
            dfar[part, :] = grads[0:BLK].astype(BF)
            down[part, :] = grads[3 * BLK :].astype(BF)
            both = grads[BLK : 3 * BLK] if both is None else both + grads[BLK : 3 * BLK]
        back[rows_at(hb * BLK, BLK), :] = both[0:BLK].astype(BF)
        back[rows_at(halo_rows + hb * BLK, BLK), :] = both[BLK:].astype(BF)
        for c, there in ((hb, below), (hblocks + hb, above)):
            part = rows_at(c * BLK, BLK)
            to_sub(back.at[part], back_in.at[part], bk_ss.at[c], bk_rs.at[c], there).start()

    def backward_weights(hb):
        parts = [rows_at((u * hblocks + hb) * BLK, BLK) for u in range(blocks // hblocks)]
        grads = jnp.concatenate([jnp.concatenate([down[p, :], dfar[p, :]], axis=1) for p in parts], axis=0)
        r = dot(jnp.concatenate([h[p, :] for p in parts], axis=0), grads, 0, 0)
        below_part = rows_at(hb * BLK, BLK)
        above_part = rows_at(halo_rows + hb * BLK, BLK)
        halo_grad = jnp.concatenate([back[below_part, :], back[above_part, :]], axis=0)
        halo_row = jnp.concatenate([halo[below_part, :], halo[above_part, :]], axis=0)
        sum_f[0:128, :] += r[:, :D]
        sum_f[128:256, :] += r[:, D:] + dot(halo_row, halo_grad, 0, 0)
        y = jnp.concatenate([upd[p, :] for p in parts], axis=0)
        sum_f[256:384, :] += dot(jnp.concatenate([summed[p, :] for p in parts], axis=0), y.astype(BF), 0, 0)
        return parts, grads, y

    def backward_latents(parts, grads, y):
        r = dot(grads, jnp.concatenate([wfs[...], wfo[...]], axis=1), 1, 1) + y
        for u, p in enumerate(parts):
            upd[p, :] = r[u * BLK : (u + 1) * BLK]

    def backward_step(hb, carry):
        backward_latents(*backward_weights(hb - 1))
        backward_edges(hb)
        return carry

    backward_edges(0)
    lax.fori_loop(1, hblocks, backward_step, 0)
    last = backward_weights(hblocks - 1)
    w_f[...] = sum_f[...].astype(BF)
    weights_scatter(w_f, rs_f, f_ss, f_rs)
    backward_latents(*last)


    f_copies = weights_line(w_f, rs_f, line_f, f_ss, f_rs, fl_ss, fl_rs)
    weights_gather(all_e, line_e, e_copies, ea_ss, ea_rs)

    for c in bk_copies:
        c.wait_recv()
    halo[0:halo_rows, :] = (dot(back_in[0:halo_rows, :], wfo[...], 1, 1) * has_above).astype(BF)
    halo[halo_rows:, :] = (dot(back_in[halo_rows:, :], wfo[...], 1, 1) * has_below).astype(BF)
    group = 1024

    def returned(i, carry):
        part = rows_at(i * group, group)
        hots = []
        for t in range(group // 256):
            row = []
            for table in (shi_v, slo_v):
                for l in range(halo_rows // 128):
                    row.append(group_hot(table[l : l + 1, :], i * (group // 256) + t))
            hots.append(jnp.concatenate(row, axis=1))
        grad_h[part, :] = (upd[part, :] + dot(jnp.concatenate(hots, axis=0), halo[...])).astype(BF)
        return carry

    def store_half(k):
        part = pl.ds(k * (rows // 2), rows // 2)
        stores.append(pltpu.make_async_copy(grad_h.at[part], grad_h_hbm.at[part], store_s.at[1 + k]))
        stores[-1].start()

    lax.fori_loop(0, rows // group // 2, returned, 0)
    store_half(0)
    weights_gather(all_f, line_f, f_copies, fa_ss, fa_rs)
    lax.fori_loop(rows // group // 2, rows // group, returned, 0)
    store_half(1)

    def finish(array, ss, rs, first, count, sem):
        size = array.shape[0] // plane
        others = array.at[pl.ds(0, array.shape[0] - size)]
        to_sub(others, others, ss, rs, above).wait_recv()
        stores.append(
            pltpu.make_async_copy(array.at[pl.ds(0, count * D)], grad_w_hbm.at[pl.ds(first * D, count * D)], sem)
        )
        stores[-1].start()

    finish(all_e, ea_ss, ea_rs, 3, 4, store_s.at[3])
    finish(all_f, fa_ss, fa_rs, 0, 3, store_s.at[4])

    for c in halo_copies + hist_copies + g_copies + t_copies + ch_copies + cb_copies:
        c.wait_send()
    for c in bk_copies + f_copies + e_copies:
        c.wait_send()
    for c in stores:
        c.wait()
    for received, array, ss, gather_ss, rs in ((rs_e, all_e, e_ss, ea_ss, e_rs), (rs_f, all_f, f_ss, fa_ss, f_rs)):
        to_sub(received, received, ss, rs, above).wait_send()
        others = array.at[pl.ds(0, array.shape[0] - array.shape[0] // plane)]
        to_sub(others, others, gather_ss, rs, above).wait_send()


def step(
    n_grp, n_sub,
    states, cotangent, fine_self, fine_other, fine_node, coarse_self, coarse_other, coarse_node, prolong,
    fine_nbr, fine_mask, fine_send_lo, fine_send_hi, coarse_nbr, coarse_mask, coarse_send_lo, coarse_send_hi, coarse_owner,
):
    rows, slots = fine_nbr.shape
    crows = coarse_nbr.shape[0]
    halo = fine_send_lo.shape[0]
    chalo = coarse_send_lo.shape[0]
    blocks, cblocks = rows // BLK, crows // BLK
    edges = BLK * slots
    vmem = pl.BlockSpec(memory_space=pltpu.VMEM)
    smem = pl.BlockSpec(memory_space=pltpu.SMEM)
    hbm = pl.BlockSpec(memory_space=pl.ANY)
    V = pltpu.VMEM
    dma = pltpu.SemaphoreType.DMA
    w_rows = 4 * D
    wc = w_rows // (n_sub // 2)
    i32 = jnp.int32
    scratch = [
        V((rows, D), BF), V((rows, D), BF), V((slots, rows), i32), V((slots, rows), i32),
        V((slots, crows), i32), V((slots, crows), i32), V((rows, D), BF), V((rows, D), BF),
        V((2 * halo, D), BF), V((2 * halo, D), BF), V((2 * halo, D), BF),
        V((rows, D), BF), V((2 * halo, D), BF), V((rows, D), BF),
        V((blocks, 8, 128), F32), V((blocks, 4 * BLK, edges), BF), V((blocks, edges, D), BF),
        V((rows // TILE, crows, TILE), BF),
        V((rows, D), BF), V((rows, D), BF), V((rows, D), F32), V((rows, D), F32), V((crows, D), F32),
        V((16, 128), F32), V((n_grp - 1, 16, 128), F32), V((crows, D), F32),
        V((crows // 2, D), BF), V((crows // 2, D), BF), V((crows // 2, D), BF), V((crows // 2, D), BF), V((crows, D), BF),
        V((crows // 2, D), BF), V((crows // 2, D), BF), V((crows // 2, D), BF), V((crows // 2, D), BF), V((crows, D), BF),
        V((crows, D), F32), V((2 * chalo, D), F32), V((2 * chalo, D), BF), V((2, 2 * chalo, D), BF), V((2 * chalo, D), BF),
        V((crows, D), BF), V((crows, D), BF), V((2 * chalo, D), BF),
        V((cblocks, 8, 128), F32), V((cblocks, 4 * BLK, edges), BF),
        V((crows, D), F32), V((crows, D), BF), V((crows, D), BF), V((crows, D), BF), V((crows, D), F32),
        V((2 * chalo, D), F32), V((2 * chalo, D), BF), V((2 * chalo, D), BF),
        V((crows, D), BF), V((crows, D), BF), V((crows, 2 * D), BF),
        V((2 * halo, D), BF), V((2 * halo, D), BF),
        V((w_rows, D), BF), V((w_rows - wc, D), BF), V((2, wc, D), BF), V((w_rows, D), BF),
        V((w_rows, D), BF), V((w_rows, D), F32), V((w_rows - wc, D), BF), V((2 * n_grp, wc, D), BF), V((w_rows, D), BF),
        dma((6,)), dma((5,)), dma((4,)), dma((4,)),
        dma((n_grp - 1,)), dma((n_grp - 1,)), dma((3,)), dma((3,)), dma((3,)), dma((3,)),
        dma((4,)), dma((4,)), dma((2,)), dma((2,)),
        dma((2 * halo // BLK,)), dma((2 * halo // BLK,)),
        dma, dma, dma((1,)), dma((1,)), dma, dma,
        dma, dma, dma((2 * n_grp - 1,)), dma((2 * n_grp - 1,)), dma, dma,
    ]
    outs = pl.pallas_call(
        functools.partial(kernel, n_grp, n_sub),
        out_shape=(
            jax.ShapeDtypeStruct((rows, D), BF),
            jax.ShapeDtypeStruct((rows, D), BF),
            jax.ShapeDtypeStruct((7 * D, D), BF),
        ),
        in_specs=[hbm] * 2 + [vmem] * 7 + [hbm] * 4 + [smem] * 4 + [vmem] * 5,
        out_specs=(hbm, hbm, hbm),
        scratch_shapes=scratch,
        compiler_params=pltpu.CompilerParams(
            collective_id=0, has_side_effects=True, vmem_limit_bytes=60 * 1024 * 1024 + 512 * 1024
        ),
    )(
        states, cotangent, fine_self, fine_other, fine_node, coarse_self, coarse_other, coarse_node, prolong,
        fine_nbr.T, fine_mask.T, coarse_nbr.T, coarse_mask.T,
        fine_send_lo, fine_send_hi, coarse_send_lo, coarse_send_hi,
        fine_send_lo.reshape(-1, 128), fine_send_hi.reshape(-1, 128),
        coarse_send_lo.reshape(1, -1), coarse_send_hi.reshape(1, -1),
        coarse_owner.reshape(-1, 128),
    )
    return copied((outs[0], outs[1], outs[2].reshape(7, D, D)), 2)


def solution(mesh):
    rows2 = P(("grp", "sub"), None)
    rows1 = P(("grp", "sub"))
    in_specs = (
        (rows2, rows2) + (P(),) * 7
        + (rows2, rows2, rows1, rows1)
        + (P("sub", None), P("sub", None), P("sub"), P("sub"), rows1)
    )
    return jax.shard_map(
        functools.partial(step, mesh.shape["grp"], mesh.shape["sub"]),
        mesh=mesh, in_specs=in_specs, out_specs=(rows2, rows2, P()), check_vma=False,
    )
```
